128 devices in a mesh: dp: 32 (over y, z, core), tp: 4 (over x).
Axes of the slice: x: 4, y: 4, z: 4, core: 2. Of those that a mesh axis runs over, the one named last changes fastest.
Arguments:
- query: bfloat16 [1024, 64, 576], P('dp', 'tp'), may hold values from -30 to 30
- cache_pool: bfloat16 [4096, 64, 576], P('dp'), may hold values from -6 to 6
- block_scale: bfloat16 [4096], P('dp'), may hold values from 0.25 to 2.5
- block_table: int32 [1024, 4], P('dp'), may hold values from 0 to 127, as said below
- lengths: int32 [1024], P('dp'), may hold values from 2 to 256, as said below
- migration: int32 [16, 3], replicated, may hold values from 0 to 1023, as said below
- value_up: bfloat16 [64, 512, 128], P('tp'), may hold values from -0.25 to 0.25
- out_weight: bfloat16 [8192, 7168], P('tp', 'dp'), may hold values from -0.0625 to 0.0625
- residual: bfloat16 [1024, 7168], P(('dp', 'tp')), may hold values from -6 to 6
- norm_gain: float32 [7168], replicated, may hold values from 0.1 to 1.9
- expert_ids: int32 [1024, 8], P(('dp', 'tp')), may hold values from 0 to 31, all different within a row; in each aligned block of 8 rows (0 to 7, 8 to 15, ...) at most 4 rows name the same one
- gate_weights: float32 [1024, 8], P(('dp', 'tp')), may hold values from 0.2 to 0.8
- expert_owner: int32 [32], replicated, may hold values from 0 to 31, each once
- w_gate: bfloat16 [32, 7168, 1024], P('dp', None, 'tp'), may hold values from -0.0625 to 0.0625
- w_up: bfloat16 [32, 7168, 1024], P('dp', None, 'tp'), may hold values from -0.0625 to 0.0625
- w_down: bfloat16 [32, 1024, 7168], P('dp', 'tp'), may hold values from -0.1875 to 0.1875
Outputs:
- mixed: bfloat16 [1024, 7168], P(('dp', 'tp'))
- arrived_blocks: bfloat16 [32, 4, 64, 576], P('dp')
- arrived_scales: bfloat16 [32, 4], P('dp')
The draws below stay inside these ranges and needn't reach their ends.
Inputs may be any that keep to these rules, and one draw needn't show every extreme that they name: `block_table`: per data rank, its 32 requests' rows together name each of its 128 local block numbers exactly once. `lengths`: some request has exactly 256 positions. `migration`: each rank is a source at most once and a destination at most once, never both; the request lives on its source rank (request // 32 equals the source); request 1024 - 1 migrates in every draw. `expert_ids`: in the rows of one device no expert is named more than 4 times.
All inputs are finite; a program needn't handle non-finite values.
Results may differ from the reference program's by a relative error of at most 0.018.
Values may be sent and summed in bfloat16 or wider, within the bound.
A program may use at most 192 MiB of HBM per device.

```python
import math
import jax
import jax.numpy as jnp
import numpy as np
from jax import lax

D = 7168
LAT = 512
ROPE = 64
VDIM = 128
TOPK = 8
HEADS = 64
FF_E = 1024
MAXB = 4
BS = 64
REQ_DP = 32
EXPERTS = 32
REQ = 1024
TOK_DEV = 8
NBLK = 128
POOL = 4096
RANKS = 32
CAP = 4
N_TP = 4


def lengths_of(key):
    key = jax.random.fold_in(key, 101)
    ranks = REQ // REQ_DP
    first, second = jax.random.split(key, 2)
    load = jax.random.randint(first, (ranks,), 1, 5)
    highest = 2 + (MAXB * BS - 2) * load // 4
    span = (highest - 1)[:, None]
    raw = jax.random.randint(second, (ranks, REQ_DP), 0, 1 << 20)
    got = 2 + raw % span
    others = jnp.max(got[:ranks - 1], axis=0)
    final_row = jnp.where(jnp.arange(REQ_DP) == REQ_DP - 1, MAXB * BS, others)
    got = got.at[ranks - 1].set(final_row)
    return got.reshape(REQ).astype(jnp.int32)


def table_of(key):
    key = jax.random.fold_in(key, 202)
    ranks = REQ // REQ_DP
    keys = jax.random.split(key, ranks)
    perms = jax.vmap(lambda k: jax.random.permutation(k, NBLK))(keys)
    return perms.reshape(REQ, MAXB).astype(jnp.int32)


def cache_of(key):
    key = jax.random.fold_in(key, 303)
    first, second = jax.random.split(key)
    base = jnp.clip(jax.random.normal(first, (POOL, BS, LAT + ROPE), jnp.float32), -6.0, 6.0)
    other = jax.random.normal(second, (POOL, LAT + ROPE), jnp.float32)
    nearby = jnp.clip(other, -6.0, 6.0)
    return base.at[:, 1].set(nearby)


def draw_lengths(key, part):
    shared = lengths_of(key)
    return shared


def draw_block_table(key, part):
    shared = table_of(key)
    return shared


def draw_cache_pool(key, part):
    values = cache_of(key)
    return values.astype(jnp.bfloat16)


def draw_query(key, part):
    key = jax.random.fold_in(key, 404)
    first = jax.random.fold_in(key, 0)
    base = jnp.clip(jax.random.normal(first, (REQ, HEADS, LAT + ROPE), jnp.float32), -6.0, 6.0)
    return base.astype(jnp.bfloat16)


def draw_migration(key, part):
    shared = lengths_of(key)
    ranks = REQ // REQ_DP
    per_rank = shared.reshape(ranks, REQ_DP)
    totals = jnp.sum(per_rank, axis=1)
    order = jnp.argsort(-(totals * ranks + jnp.arange(ranks)))
    heavy = order[:ranks // 2]
    light = order[ranks // 2:][::-1]
    picked = per_rank[heavy] * REQ_DP + jnp.arange(REQ_DP)[None, :]
    within = jnp.argmax(picked, axis=1)
    movers = heavy * REQ_DP + within
    return jnp.stack([movers, heavy, light], axis=1).astype(jnp.int32)


def levels(rng, dims, cuts, least, largest):
    gain = 1.0
    for dim, blocks in cuts:
        heights = jax.random.uniform(jax.random.fold_in(jax.random.fold_in(rng, 6), dim), (blocks,), jnp.float32, least / len(cuts), largest / len(cuts))
        gain = gain * jnp.repeat(jnp.exp(heights), dims[dim] // blocks).reshape((-1,) + (1,) * (len(dims) - 1 - dim))
    return gain


def shared_out(rng, own, number, rows, amount, top, limit, skew):
    sequence = jax.random.permutation(rng, amount)
    crowded, usual = load_shares(amount, rows * top, limit, skew, True), load_shares(amount, rows * top, limit, skew, False)
    places = jnp.arange(amount)

    def named(sizes, offset_by):
        used = int((sizes > 0).sum())
        fixed = max(1, used // 4)
        shifted = fixed + (places - fixed + offset_by * (used - fixed)) % max(1, amount - fixed)
        return jnp.zeros((amount,), jnp.int32).at[sequence[jnp.where(places < fixed, places, shifted)]].set(jnp.asarray(sizes, jnp.int32))

    sizes = jnp.where(number % 4 == 0, named(crowded, number // 4), named(usual, number - number // 4 - 1))
    mixed = jax.random.permutation(jax.random.fold_in(own, 3), amount)
    source_of, receiver = mixed[0:amount // 2 * 2:2], mixed[1:amount // 2 * 2:2]
    margin = jnp.minimum(sizes[source_of] - 1, limit - sizes[receiver]) // 2
    margin = jnp.where((source_of == sequence[0]) | (receiver == sequence[0]) | (sizes[receiver] == 0), 0, jnp.maximum(margin, 0))
    shifted = jax.random.randint(jax.random.fold_in(own, 4), (amount // 2,), 0, 1 << 20) % (margin + 1)
    sizes = sizes.at[source_of].add(-shifted).at[receiver].add(shifted)
    labels = jnp.searchsorted(jnp.cumsum(sizes), jnp.arange(rows * top), side="right").astype(jnp.int32)
    table = labels.reshape(top, rows).T
    table = table[jax.random.permutation(jax.random.fold_in(own, 1), rows)]
    offset_by = jax.random.randint(jax.random.fold_in(own, 2), (rows, 1), 0, top)
    return jnp.take_along_axis(table, (jnp.arange(top)[None, :] + offset_by) % top, axis=1)


def load_shares(number_of, total, most, skew, full):
    weights = [(1 << 20) // math.isqrt(grade ** skew) + 1 for grade in range(1, number_of + 1)]
    largest = most if full else min(most, max(-(-total // number_of), total * weights[0] // sum(weights)))
    least = 1 if total - largest >= number_of - 1 else 0
    given, spare = [largest] + [least] * (number_of - 1), total - largest - least * (number_of - 1)
    while spare > 0:
        free = [i for i in range(1, number_of) if given[i] < largest] or [i for i in range(1, number_of) if given[i] < most]
        whole, left = sum([weights[i] for i in free]), spare
        for i in free:
            more = min(most - given[i], max(1, left * weights[i] // whole), spare)
            given[i] = given[i] + more
            spare = spare - more
    return np.array(given)


def centred(own_key, dims, scale, reach, shards=(), kind=jnp.bfloat16):
    gain = levels(own_key, dims, shards, -0.22, 0.18) if shards else 1.0
    entries = jax.random.normal(own_key, dims, jnp.float32) * scale * gain
    return jnp.minimum(jnp.maximum(entries, -reach), reach).astype(kind)


def setup_inputs(seed: int = 0) -> dict:
    splits = jax.random.split(jax.random.key(seed), 17)
    query = draw_query(jax.random.fold_in(splits[16], 71), 0)
    cache_pool = draw_cache_pool(jax.random.fold_in(splits[16], 71), 0)
    block_scale = jnp.clip(jnp.exp(math.log(2.5) - 2.3025851 * jax.random.uniform(splits[2], (POOL,), jnp.float32) ** levels(splits[2], (POOL,), ((0, 32),), -0.2, 0.2)), 0.25, 2.5).astype(jnp.bfloat16)
    block_table = draw_block_table(jax.random.fold_in(splits[16], 71), 0)
    lengths = draw_lengths(jax.random.fold_in(splits[16], 71), 0)
    migration = draw_migration(jax.random.fold_in(splits[16], 71), 0)
    value_up = centred(splits[6], (HEADS, LAT, VDIM), LAT ** -0.5, 0.25, ((0, 4),))
    out_weight = centred(splits[7], (HEADS * VDIM, D), (HEADS * VDIM) ** -0.5, 0.0625, ((0, 4), (1, 32)))
    residual = centred(splits[8], (REQ, D), 1.0, 6.0, ((0, 128),))
    norm_gain = jnp.clip(1.0 + 0.18 * jax.random.normal(splits[9], (D,), jnp.float32), 0.1, 1.9)
    expert_ids_keys = jax.random.split(jax.random.fold_in(splits[10], 1), REQ // TOK_DEV)
    expert_ids_turns = jax.random.permutation(jax.random.fold_in(splits[10], 3), REQ // TOK_DEV)
    expert_ids = jax.vmap(lambda own, number: shared_out(jax.random.fold_in(splits[10], 2), own, number, TOK_DEV, EXPERTS, TOPK, CAP, 2))(expert_ids_keys, expert_ids_turns).reshape((REQ, TOPK))
    gate_weights = jnp.clip(0.2 + 0.6 * jax.random.uniform(splits[11], (REQ, TOPK), jnp.float32) ** levels(splits[11], (REQ, TOPK), ((0, 128),), -0.2, 0.2), 0.2, 0.8)
    expert_owner = jax.random.permutation(splits[12], EXPERTS).astype(jnp.int32)
    w_gate = centred(splits[13], (RANKS, D, FF_E), D ** -0.5, 0.0625, ((0, 32), (2, 4)))
    w_up = centred(splits[14], (RANKS, D, FF_E), D ** -0.5, 0.0625, ((0, 32), (2, 4)))
    w_down = centred(splits[15], (RANKS, FF_E, D), FF_E ** -0.5, 0.1875, ((0, 32), (1, 4)))
    return {"query": query, "cache_pool": cache_pool, "block_scale": block_scale, "block_table": block_table, "lengths": lengths, "migration": migration, "value_up": value_up, "out_weight": out_weight, "residual": residual, "norm_gain": norm_gain, "expert_ids": expert_ids, "gate_weights": gate_weights, "expert_owner": expert_owner, "w_gate": w_gate, "w_up": w_up, "w_down": w_down}


softmax_scale = 192.0 ** (-0.5)
norm_eps = 1e-06

def attend_rank(query, pool, scales, table, lengths, value_up):
    requests = table.shape[0]
    tiles = pool[table].reshape(requests, MAXB * BS, LAT + ROPE)
    pos_scale = jnp.repeat(scales[table].astype(jnp.float32), BS, axis=1)
    scores = jnp.einsum('rhc,rpc->rhp', query.astype(jnp.float32), tiles.astype(jnp.float32))
    scores = scores * softmax_scale * pos_scale[:, None, :]
    live = jnp.arange(MAXB * BS)[None, :] < lengths[:, None]
    scores = jnp.where(live[:, None, :], scores, -1e+30)
    top = lax.optimization_barrier(jnp.max(scores, axis=2, keepdims=True))
    expo = jnp.exp(scores - top)
    weight = expo / lax.optimization_barrier(jnp.sum(expo, axis=2, keepdims=True))
    coef = (weight * pos_scale[:, None, :]).astype(jnp.bfloat16)
    latent_out = jnp.einsum('rhp,rpc->rhc', coef.astype(jnp.float32), tiles[:, :, :LAT].astype(jnp.float32)).astype(jnp.bfloat16)
    head_out = jnp.einsum('rhc,hcv->rhv', latent_out.astype(jnp.float32), value_up.astype(jnp.float32)).astype(jnp.bfloat16)
    return head_out.reshape(requests, HEADS * VDIM)

def reference(query, cache_pool, block_scale, block_table, lengths, migration, value_up, out_weight, residual, norm_gain, expert_ids, gate_weights, expert_owner, w_gate, w_up, w_down):
    ranks = REQ // REQ_DP
    queries = query.reshape(ranks, REQ_DP, HEADS, LAT + ROPE)
    pools = cache_pool.reshape(ranks, NBLK, BS, LAT + ROPE)
    scales = block_scale.reshape(ranks, NBLK)
    tables = block_table.reshape(ranks, REQ_DP, MAXB)
    lens = lengths.reshape(ranks, REQ_DP)

    def one_rank(items):
        return attend_rank(items[0], items[1], items[2], items[3], items[4], value_up)
    head_out = lax.map(one_rank, (queries, pools, scales, tables, lens)).reshape(REQ, HEADS * VDIM)
    proj = jnp.dot(head_out, out_weight, preferred_element_type=jnp.float32).astype(jnp.bfloat16)
    stream = residual.astype(jnp.float32) + proj.astype(jnp.float32)
    power = lax.optimization_barrier(jnp.mean(stream * stream, axis=1, keepdims=True))
    normed = (stream * lax.rsqrt(power + norm_eps) * norm_gain[None, :]).astype(jnp.bfloat16)

    def one_expert(total, expert):
        slot = expert_owner[expert]
        gate = jnp.dot(normed, w_gate[slot], preferred_element_type=jnp.float32)
        upper = jnp.dot(normed, w_up[slot], preferred_element_type=jnp.float32)
        hidden = (jax.nn.silu(gate) * upper).astype(jnp.bfloat16)
        blocks = hidden.reshape(REQ, N_TP, FF_E // N_TP).astype(jnp.float32)
        down = w_down[slot].reshape(N_TP, FF_E // N_TP, D).astype(jnp.float32)
        partial_value = jnp.einsum('tnf,nfd->tnd', blocks, down).astype(jnp.bfloat16)
        result = lax.optimization_barrier(jnp.sum(partial_value.astype(jnp.float32), axis=1))
        chosen = lax.optimization_barrier(jnp.sum(jnp.where(expert_ids == expert, gate_weights, 0.0), axis=1))
        return (total + chosen[:, None] * result, None)
    moe, _ = lax.scan(one_expert, jnp.zeros((REQ, D), jnp.float32), jnp.arange(EXPERTS))
    mixed = (stream + moe).astype(jnp.bfloat16)
    movers = migration[:, 0]
    sources = migration[:, 1]
    targets = migration[:, 2]
    rows = block_table[movers]
    blocks = (sources[:, None] * NBLK + rows).astype(jnp.int32)
    arrived_blocks = jnp.zeros((ranks, MAXB, BS, LAT + ROPE), jnp.bfloat16).at[targets].set(cache_pool[blocks])
    arrived_scales = jnp.zeros((ranks, MAXB), jnp.bfloat16).at[targets].set(block_scale[blocks])
    return (mixed, arrived_blocks, arrived_scales)
```

```python
import functools
import jax
import jax.numpy as jnp
from jax import lax
from jax.experimental import pallas as pl
from jax.experimental.pallas import tpu as pltpu
from jax.sharding import PartitionSpec as P

softmax_scale = 192.0 ** (-0.5)
MESH = pl.DeviceIdType.MESH
norm_eps = 1e-06
WIDE = 7168
HALF = 3584
PARTS = ((0, 1280), (1280, 1280), (2560, 1024))
ORDER = ((0, 1, 2), (1, 2, 0), (2, 0, 1))
TILE = 256


class Links:
    def __init__(self, send, recv):
        self.send, self.recv, self.used = send, recv, 0
        rank = lax.axis_index("dp")
        self.core = lax.rem(rank, 2)
        self.pos = (lax.axis_index("tp"), rank // 8, lax.rem(rank // 2, 4))

    def device(self, pos, core):
        return ((pos[1] * 4 + pos[2]) * 2 + core, pos[0])

    def along(self, axis, step):
        return lax.rem(self.pos[axis] + step, 4)

    def near(self, axis, step):
        pos = list(self.pos)
        pos[axis] = self.along(axis, step)
        return self.device(pos, self.core)

    def twin(self):
        return self.device(self.pos, 1 - self.core)

    def copy(self, src, dst, device):
        slot = self.used
        self.used += 1
        made = pltpu.make_async_remote_copy(
            src_ref=src,
            dst_ref=dst,
            send_sem=self.send.at[slot],
            recv_sem=self.recv.at[slot],
            device_id=device,
            device_id_type=MESH,
        )
        made.start()
        return made


def place(part, a, b, c):
    index = [None, None, None]
    for axis, value in zip(ORDER[part], (a, b, c)):
        index[axis] = value
    return tuple(index)


ALL = slice(None)


def expert_kernel(
    s16, gain, coef, wg_in, wu_in, wd_in, out,
    x0, x1, x2, t0, t1, t2, wg, wu, wd, accg, accu, hid,
    r0, r1, r2, ca0, ca1, ca2, cb0, cb1, cb2, bb0, bb1, bb2, aa0, aa1, aa2,
    sums, fin, load, send, recv,
):
    net = Links(send, recv)
    core = net.core
    x, t, r = (x0, x1, x2), (t0, t1, t2), (r0, r1, r2)
    ca, cb, bb, aa = (ca0, ca1, ca2), (cb0, cb1, cb2), (bb0, bb1, bb2), (aa0, aa1, aa2)

    barrier = pltpu.get_barrier_semaphore()
    partners = [net.near(axis, k) for axis in range(3) for k in (1, 3, 2)] + [net.twin()]
    for device in partners:
        pl.semaphore_signal(barrier, inc=1, device_id=device, device_id_type=MESH)

    loads = []
    for half in range(2):
        which = core if half == 0 else 1 - core
        rows = pl.ds(pl.multiple_of(which * HALF, HALF), HALF)
        for n, (src, dst) in enumerate(
            ((wg_in.at[0, rows, :], wg.at[half]), (wu_in.at[0, rows, :], wu.at[half]), (wd_in.at[0, :, rows], wd.at[half]))
        ):
            made = pltpu.make_async_copy(src, dst, load.at[half * 3 + n])
            made.start()
            loads.append(made)

    stream = s16[...]
    power = jnp.sum(stream * stream, axis=1, keepdims=True)
    sums[0] = jnp.broadcast_to(power, (16, 128))
    pl.semaphore_wait(barrier, len(partners))
    pair = net.copy(sums.at[0], sums.at[1], net.twin())
    accg[...] = jnp.zeros_like(accg)
    accu[...] = jnp.zeros_like(accu)
    pair.wait()
    power = (sums[0][:, 0:1] + sums[1][:, 0:1]) * (1.0 / WIDE)
    scale = lax.rsqrt(power + norm_eps)
    px, py, pz = net.pos
    sent = []

    def go(src, dst, device):
        made = net.copy(src, dst, device)
        sent.append(made)
        return made

    pa, pb, pc = [], [], []
    for p, (off, width) in enumerate(PARTS):
        cols = slice(off, off + width)
        x[p][px, py, pz] = (s16[:, cols] * scale * gain[core][:, cols]).astype(jnp.bfloat16)
    ga = []
    for p in range(3):
        block = x[p].at[px, py, pz]
        ga.append([go(block, block, net.near(ORDER[p][0], k)) for k in (1, 3, 2)])

    JS = (0, 1, 3, 2)
    SLOT = {1: 1, 3: 0, 2: 2}
    gb = [None] * 3
    gc = [[None] * 4 for _ in range(3)]
    gf = [[None] * 4 for _ in range(3)]
    twins = []

    def line(p, ref, jb, jc):
        return ref.at[place(p, ALL, net.along(ORDER[p][1], jb), net.along(ORDER[p][2], jc))]

    def to_twin(p, jb, jc):
        made = go(line(p, x[p], jb, jc), line(p, t[p], jb, jc), net.twin())
        twins.append((p, jb, jc, made))

    def spread(p, n):
        src = line(p, x[p], JS[n], 0)
        gc[p][n] = [go(src, src, net.near(ORDER[p][2], k)) for k in (1, 3)]
        to_twin(p, JS[n], 0)

    def multiply(p, ref, jc, half):
        off, width = PARTS[p]
        where = place(p, ALL, ALL, net.along(ORDER[p][2], jc))

        def step(k, carry):
            lanes = pl.ds(pl.multiple_of(k * TILE, TILE), TILE)
            rows = pl.ds(pl.multiple_of(off + k * TILE, TILE), TILE)
            left = ref[where + (ALL, lanes)].reshape(256, TILE)
            accg[where] += jnp.dot(left, wg[half, rows, :], preferred_element_type=jnp.float32).reshape(4, 4, 16, 256)
            accu[where] += jnp.dot(left, wu[half, rows, :], preferred_element_type=jnp.float32).reshape(4, 4, 16, 256)
            return carry

        lax.fori_loop(0, width // TILE, step, 0)

    for p in range(3):
        for made in ga[p]:
            made.wait_recv()
        src = line(p, x[p], 0, 0)
        gb[p] = [go(src, src, net.near(ORDER[p][1], k)) for k in (1, 3, 2)]
        spread(p, 0)
    for made in loads:
        made.wait()
    for n in (1, 2, 3):
        for p in range(3):
            gb[p][SLOT[JS[n]]].wait_recv()
            spread(p, n)
    for n in range(4):
        for p in range(3):
            gc[p][n][0].wait_recv()
            gc[p][n][1].wait_recv()
            if n % 2 == 0:
                src = line(p, x[p], JS[n], 3)
                gf[p][n] = go(src, src, net.near(ORDER[p][2], 1))
            else:
                src = line(p, x[p], JS[n], 1)
                gf[p][n] = go(src, src, net.near(ORDER[p][2], 3))
            to_twin(p, JS[n], 3)
            to_twin(p, JS[n], 1)
            if n == 0:
                multiply(p, x[p], 0, 0)
            if n == 1:
                for q, jb, jc, made in twins:
                    if q == p and jc == 0:
                        made.wait_recv()
                multiply(p, t[p], 0, 1)
    for p in range(3):
        multiply(p, x[p], 1, 0)
        multiply(p, x[p], 3, 0)
        for jc in (1, 3):
            for q, jb, kc, made in twins:
                if q == p and kc == jc:
                    made.wait_recv()
            multiply(p, t[p], jc, 1)
    for p in range(3):
        for n in range(4):
            gf[p][n].wait_recv()
            to_twin(p, JS[n], 2)
        multiply(p, x[p], 2, 0)
    for p in range(3):
        for q, jb, kc, made in twins:
            if q == p and kc == 2:
                made.wait_recv()
        multiply(p, t[p], 2, 1)
    for made in sent:
        made.wait_send()
    sent.clear()

    def activate(k, carry):
        g = accg[k].reshape(256, 256)
        u = accu[k].reshape(256, 256)
        c = coef[k].reshape(256, 128)[:, 0:1]
        hid[k] = (g * jax.nn.sigmoid(g) * u * c).astype(jnp.bfloat16).reshape(4, 4, 16, 256)
        return carry

    lax.fori_loop(0, 4, activate, 0)

    def down_twin(p, jc):
        off, width = PARTS[p]
        where = place(p, ALL, ALL, net.along(ORDER[p][2], jc))

        def step(k, carry):
            lanes = pl.ds(pl.multiple_of(k * TILE, TILE), TILE)
            cols = pl.ds(pl.multiple_of(off + k * TILE, TILE), TILE)
            got = jnp.dot(hid[where].reshape(256, 256), wd[1, :, cols], preferred_element_type=jnp.float32)
            t[p][where + (ALL, lanes)] = got.astype(jnp.bfloat16).reshape(4, 4, 16, TILE)
            return carry

        lax.fori_loop(0, width // TILE, step, 0)
        return go(t[p].at[where], r[p].at[where], net.twin())

    def down_own(p, jc, made):
        off, width = PARTS[p]
        where = place(p, ALL, ALL, net.along(ORDER[p][2], jc))
        made.wait_recv()

        def step(k, carry):
            lanes = pl.ds(pl.multiple_of(k * TILE, TILE), TILE)
            cols = pl.ds(pl.multiple_of(off + k * TILE, TILE), TILE)
            got = jnp.dot(hid[where].reshape(256, 256), wd[0, :, cols], preferred_element_type=jnp.float32)
            got = got + r[p][where + (ALL, lanes)].reshape(256, TILE).astype(jnp.float32)
            x[p][where + (ALL, lanes)] = got.astype(jnp.bfloat16).reshape(4, 4, 16, TILE)
            return carry

        lax.fori_loop(0, width // TILE, step, 0)

    JB = (2, 1, 3, 0)
    PLUS, MINUS = (0, 3), (1, 2)
    steps = [(p, jc) for jc in (2, 1, 3, 0) for p in range(3)]
    made_twin = {}
    h1, h2 = {}, {}

    def add_line(p, jb, jc, others):
        b, c = net.along(ORDER[p][1], jb), net.along(ORDER[p][2], jc)

        def step(k, carry):
            where = place(p, k, b, c)
            total = x[p][where].astype(jnp.float32)
            for ref, index in others:
                total = total + ref[index + (k,)].astype(jnp.float32)
            x[p][where] = total.astype(jnp.bfloat16)
            return carry

        lax.fori_loop(0, 4, step, 0)

    def send_c1(p):
        h1[p] = []
        for i, n in enumerate(PLUS):
            h1[p].append(go(line(p, x[p], JB[n], 2), ca[p].at[0, i], net.near(ORDER[p][2], 1)))
        for i, n in enumerate(MINUS):
            h1[p].append(go(line(p, x[p], JB[n], 2), ca[p].at[1, i], net.near(ORDER[p][2], 3)))

    def send_c2(p, jc):
        way = 0 if jc == 1 else 1
        mine = PLUS if jc == 1 else MINUS
        for i in range(2):
            h1[p][way * 2 + i].wait_recv()
        for n in range(4):
            if n in mine:
                add_line(p, JB[n], jc, [(ca[p], (way, mine.index(n)))])
            h2[p, way, n] = go(line(p, x[p], JB[n], jc), cb[p].at[way, n], net.near(ORDER[p][2], jc))

    made_twin[steps[0]] = down_twin(*steps[0])
    for i, (p, jc) in enumerate(steps):
        if i + 1 < len(steps):
            made_twin[steps[i + 1]] = down_twin(*steps[i + 1])
        down_own(p, jc, made_twin[p, jc])
        if jc == 2:
            send_c1(p)
        elif jc != 0:
            send_c2(p, jc)
    hb = [[None] * 4 for _ in range(3)]
    for n in range(3):
        for p in range(3):
            for way in range(2):
                h2[p, way, n].wait_recv()
            add_line(p, JB[n], 0, [(cb[p], (0, n)), (cb[p], (1, n))])
            hb[p][n] = go(line(p, x[p], JB[n], 0), bb[p].at[n], net.near(ORDER[p][1], JB[n]))
    for p in range(3):
        for way in range(2):
            h2[p, way, 3].wait_recv()
        for n in range(3):
            hb[p][n].wait_recv()
        add_line(p, 0, 0, [(cb[p], (0, 3)), (cb[p], (1, 3))] + [(bb[p], (n,)) for n in range(3)])
    haa = []
    for p in range(3):
        _, mb, mc = (net.pos[axis] for axis in ORDER[p])
        for n, k in enumerate((2, 1, 3)):
            src = x[p].at[place(p, net.along(ORDER[p][0], k), mb, mc)]
            haa.append(go(src, aa[p].at[n], net.near(ORDER[p][0], k)))
    for p, (off, width) in enumerate(PARTS):
        for n in range(3):
            haa[p * 3 + n].wait_recv()
        total = x[p][px, py, pz].astype(jnp.float32)
        for n in range(3):
            total = total + aa[p][n].astype(jnp.float32)
        fin[0, :, off:off + width] = s16[:, off:off + width] + total
    theirs = fin.at[0, pl.ds(pl.multiple_of((1 - core) * 8, 8), 8)]
    last = net.copy(theirs, fin.at[1, pl.ds(0, 8)], net.twin())
    mine = fin[0, pl.ds(pl.multiple_of(core * 8, 8), 8)]
    out[:, pl.ds(pl.multiple_of(core * HALF, HALF), HALF)] = mine.astype(jnp.bfloat16)
    last.wait_recv()
    out[:, pl.ds(pl.multiple_of((1 - core) * HALF, HALF), HALF)] = fin[1, 0:8].astype(jnp.bfloat16)
    last.wait_send()
    for made in sent:
        made.wait_send()


def experts(s16, gain, coef, w_gate, w_up, w_down):
    bf = jnp.bfloat16
    slots = 180
    vm = pl.BlockSpec(memory_space=pltpu.VMEM)
    hbm = pl.BlockSpec(memory_space=pl.ANY)
    grid = [pltpu.VMEM((4, 4, 4, 16, w), bf) for _, w in PARTS]
    return pl.pallas_call(
        expert_kernel,
        out_shape=jax.ShapeDtypeStruct((8, WIDE), bf),
        in_specs=[vm, vm, vm, hbm, hbm, hbm],
        out_specs=vm,
        scratch_shapes=grid + grid + [
            pltpu.VMEM((2, HALF, 256), bf),
            pltpu.VMEM((2, HALF, 256), bf),
            pltpu.VMEM((2, 256, HALF), bf),
            pltpu.VMEM((4, 4, 4, 16, 256), jnp.float32),
            pltpu.VMEM((4, 4, 4, 16, 256), jnp.float32),
            pltpu.VMEM((4, 4, 4, 16, 256), bf),
        ] + grid
        + [pltpu.VMEM((2, 2, 4, 16, w), bf) for _, w in PARTS]
        + [pltpu.VMEM((2, 4, 4, 16, w), bf) for _, w in PARTS]
        + [pltpu.VMEM((3, 4, 16, w), bf) for _, w in PARTS]
        + [pltpu.VMEM((3, 16, w), bf) for _, w in PARTS]
        + [
            pltpu.VMEM((2, 16, 128), jnp.float32),
            pltpu.VMEM((2, 16, HALF), jnp.float32),
            pltpu.SemaphoreType.DMA((6,)),
            pltpu.SemaphoreType.DMA((slots,)),
            pltpu.SemaphoreType.DMA((slots,)),
        ],
        compiler_params=pltpu.CompilerParams(collective_id=2, has_side_effects=True, vmem_limit_bytes=62 * 2**20),
        name="experts",
    )(s16, gain.reshape(2, 1, HALF), coef, w_gate, w_up, w_down)


def attend(query, cache_pool, block_scale, block_table, lengths, value_up):
    requests = block_table.shape[0]
    block_size = cache_pool.shape[1]
    latent = value_up.shape[1]
    context = block_table.shape[1] * block_size
    tiles = cache_pool[block_table].reshape(requests, context, cache_pool.shape[2])
    pos_scale = jnp.repeat(block_scale[block_table].astype(jnp.float32), block_size, axis=1)
    scores = jnp.einsum("rhc,rpc->rhp", query, tiles, preferred_element_type=jnp.float32)
    scores = scores * softmax_scale * pos_scale[:, None, :]
    live = jnp.arange(context)[None, :] < lengths[:, None]
    scores = jnp.where(live[:, None, :], scores, -1e30)
    top = jnp.max(scores, axis=2, keepdims=True)
    expo = jnp.exp(scores - top)
    weight = expo / jnp.sum(expo, axis=2, keepdims=True)
    coef = (weight * pos_scale[:, None, :]).astype(jnp.bfloat16)
    latent_out = jnp.einsum(
        "rhp,rpc->rhc", coef, tiles[:, :, :latent], preferred_element_type=jnp.float32
    ).astype(jnp.bfloat16)
    head_out = jnp.einsum(
        "rhc,hcv->rhv", latent_out, value_up, preferred_element_type=jnp.float32
    ).astype(jnp.bfloat16)
    return head_out.reshape(requests, -1)


def body(
    query,
    cache_pool,
    block_scale,
    block_table,
    lengths,
    migration,
    value_up,
    out_weight,
    residual,
    norm_gain,
    expert_ids,
    gate_weights,
    expert_owner,
    w_gate,
    w_up,
    w_down,
):
    ranks = lax.axis_size("dp")
    rank = lax.axis_index("dp")
    requests = block_table.shape[0]
    leaving = migration[:, 1] == rank
    local_req = jnp.sum(jnp.where(leaving, migration[:, 0] - rank * requests, 0))
    is_source = jnp.any(leaving)
    out_rows = lax.dynamic_index_in_dim(block_table, local_req, 0, keepdims=False)
    out_blocks = jnp.where(is_source, cache_pool[out_rows], 0)[None]
    out_scales = jnp.where(is_source, block_scale[out_rows], 0)[None]
    coming = migration[:, 2] == rank
    sender = jnp.sum(jnp.where(coming, migration[:, 1], 0))
    has_in = jnp.any(coming)
    empty = (
        jnp.zeros(out_blocks.shape[1:], jnp.bfloat16),
        jnp.zeros(out_scales.shape[1:], jnp.bfloat16),
    )
    blocks = lax.all_gather(out_blocks, "dp", axis=0, tiled=True)
    scales = lax.all_gather(out_scales, "dp", axis=0, tiled=True)
    inside = has_in & (sender >= 0) & (sender < blocks.shape[0])
    chosen = jnp.clip(sender, 0, blocks.shape[0] - 1)
    pick_blocks = lax.dynamic_index_in_dim(blocks, chosen, 0, keepdims=False)
    pick_scales = lax.dynamic_index_in_dim(scales, chosen, 0, keepdims=False)
    arrived_blocks = jnp.where(inside, pick_blocks, empty[0])
    arrived_scales = jnp.where(inside, pick_scales, empty[1])
    head_out = attend(query, cache_pool, block_scale, block_table, lengths, value_up)
    columns = out_weight.shape[1]
    partial_value = jnp.dot(
        lax.all_gather(head_out, "dp", axis=0, tiled=True),
        out_weight,
        preferred_element_type=jnp.float32,
    )
    summed = lax.psum_scatter(
        partial_value.reshape(ranks, requests, columns).astype(jnp.bfloat16),
        "tp",
        scatter_dimension=1,
        tiled=True,
    )
    landed = lax.all_to_all(summed, "dp", split_axis=0, concat_axis=2, tiled=True)
    proj = landed.reshape(landed.shape[1], landed.shape[2])
    stream = residual.astype(jnp.float32) + proj.astype(jnp.float32)
    groups = [[2 * i, 2 * i + 1] for i in range(16)]
    s16 = lax.all_to_all(
        stream.reshape(8, 2, HALF), "dp", split_axis=1, concat_axis=0, axis_index_groups=groups, tiled=True
    ).reshape(16, HALF)
    owners = expert_owner[expert_ids]
    picks = owners[:, :, None] == jnp.arange(ranks)[None, None, :]
    shares = jnp.sum(jnp.where(picks, gate_weights[:, :, None], 0.0), axis=1)
    shares = lax.all_gather(shares, ("dp", "tp"), axis=0, tiled=True)
    coef = lax.dynamic_index_in_dim(shares, rank, 1, keepdims=False)
    coef = coef.reshape(4, 4, 2, 4, 8).transpose(3, 0, 1, 2, 4).reshape(4, 4, 4, 16, 1)
    coef = jnp.broadcast_to(coef, (4, 4, 4, 16, 128))
    mixed = experts(s16, norm_gain, coef, w_gate, w_up, w_down)
    return (mixed, arrived_blocks[None], arrived_scales[None])


def solution(mesh):
    return jax.shard_map(
        body,
        mesh=mesh,
        in_specs=(
            P("dp", "tp", None),
            P("dp", None, None),
            P("dp"),
            P("dp", None),
            P("dp"),
            P(),
            P("tp", None, None),
            P("tp", "dp"),
            P(("dp", "tp"), None),
            P(),
            P(("dp", "tp"), None),
            P(("dp", "tp"), None),
            P(),
            P("dp", None, "tp"),
            P("dp", None, "tp"),
            P("dp", "tp", None),
        ),
        out_specs=(P(("dp", "tp"), None), P("dp", None, None, None), P("dp", None)),
        check_vma=False,
    )
```

```python
import functools
import jax
import jax.numpy as jnp
from jax import lax
from jax.experimental import pallas as pl
from jax.experimental.pallas import tpu as pltpu
from jax.sharding import PartitionSpec as P

MESH = pl.DeviceIdType.MESH
norm_eps = 1e-06
WIDE = 7168
HALF = 3584
PARTS = ((0, 1280), (1280, 1280), (2560, 1024))
GRIDS = (1280, 1280, 1152)
ORDER = ((0, 1, 2), (1, 2, 0), (2, 0, 1))
TILE = 256


class Links:
    def __init__(self, send, recv):
        self.send, self.recv, self.used = send, recv, 0
        rank = lax.axis_index("dp")
        self.core = lax.rem(rank, 2)
        self.pos = (lax.axis_index("tp"), rank // 8, lax.rem(rank // 2, 4))

    def device(self, pos, core):
        return ((pos[1] * 4 + pos[2]) * 2 + core, pos[0])

    def along(self, axis, step):
        return lax.rem(self.pos[axis] + step, 4)

    def near(self, axis, step):
        pos = list(self.pos)
        pos[axis] = self.along(axis, step)
        return self.device(pos, self.core)

    def twin(self):
        return self.device(self.pos, 1 - self.core)

    def copy(self, src, dst, device):
        slot = self.used
        self.used += 1
        made = pltpu.make_async_remote_copy(
            src_ref=src,
            dst_ref=dst,
            send_sem=self.send.at[slot],
            recv_sem=self.recv.at[slot],
            device_id=device,
            device_id_type=MESH,
        )
        made.start()
        return made


def place(part, a, b, c):
    index = [None, None, None]
    for axis, value in zip(ORDER[part], (a, b, c)):
        index[axis] = value
    return tuple(index)


ALL = slice(None)


def expert_kernel(
    s16, gain, ids, gates, owner, wg_in, wu_in, wd_in, out,
    x0, x1, x2, t0, t1, t2, wg, wu, wd, accg, accu, hid,
    r0, r1, r2, ca0, ca1, ca2, cb0, cb1, cb2, bb0, bb1, bb2, aa0, aa1, aa2,
    sums, both, fin, load, send, recv,
):
    net = Links(send, recv)
    core = net.core
    x, t, r = (x0, x1, x2), (t0, t1, t2), (r0, r1, r2)
    ca, cb, bb, aa = (ca0, ca1, ca2), (cb0, cb1, cb2), (bb0, bb1, bb2), (aa0, aa1, aa2)

    barrier = pltpu.get_barrier_semaphore()
    partners = [net.near(axis, k) for axis in range(3) for k in (1, 3, 2)] + [net.twin()]
    for device in partners:
        pl.semaphore_signal(barrier, inc=1, device_id=device, device_id_type=MESH)

    loads = []
    for half in range(2):
        which = core if half == 0 else 1 - core
        rows = pl.ds(pl.multiple_of(which * HALF, HALF), HALF)
        for n, (src, dst) in enumerate(
            ((wg_in.at[0, rows, :], wg.at[half]), (wu_in.at[0, rows, :], wu.at[half]), (wd_in.at[0, :, rows], wd.at[half]))
        ):
            made = pltpu.make_async_copy(src, dst, load.at[half * 3 + n])
            made.start()
            loads.append(made)

    stream = s16[...]
    power = jnp.sum(stream * stream, axis=1, keepdims=True)
    sums[0, 0:16] = jnp.broadcast_to(power, (16, 128))
    lane = lax.broadcasted_iota(jnp.int32, (1, 128), 1)
    held = jnp.full((1, 128), -1, jnp.int32)
    for e in range(32):
        at = owner[e]
        held = jnp.where(jnp.logical_or(lane == at, lane == at + 32), e, held)
    share = jnp.zeros((8, 128), jnp.float32)
    for k in range(8):
        share = share + jnp.where(ids[:, k:k + 1] == held, gates[:, k:k + 1], 0.0)
    sums[0, 16:24] = share
    both[pl.ds(pl.multiple_of(core * 8, 8), 8)] = share
    pl.semaphore_wait(barrier, len(partners))
    pair = net.copy(sums.at[0], sums.at[1], net.twin())
    accg[...] = jnp.zeros_like(accg)
    accu[...] = jnp.zeros_like(accu)
    pair.wait()
    power = (sums[0, 0:16][:, 0:1] + sums[1, 0:16][:, 0:1]) * (1.0 / WIDE)
    scale = lax.rsqrt(power + norm_eps)
    both[pl.ds(pl.multiple_of((1 - core) * 8, 8), 8)] = sums[1, 16:24]
    share = both[...]
    high = share.astype(jnp.bfloat16)
    rest = (share - high.astype(jnp.float32)).astype(jnp.bfloat16)
    px, py, pz = net.pos
    x[2][px, py, pz, :, 1024:1152] = jnp.where(lane < 32, high, rest)
    sent = []

    def go(src, dst, device):
        made = net.copy(src, dst, device)
        sent.append(made)
        return made

    for p, (off, width) in enumerate(PARTS):
        cols = slice(off, off + width)
        x[p][px, py, pz, :, 0:width] = (s16[:, cols] * scale * gain[core][:, cols]).astype(jnp.bfloat16)
    ga = []
    for p in range(3):
        block = x[p].at[px, py, pz]
        ga.append([go(block, block, net.near(ORDER[p][0], k)) for k in (1, 3, 2)])

    JS = (0, 1, 3, 2)
    SLOT = {1: 1, 3: 0, 2: 2}
    gb = [None] * 3
    gc = [[None] * 4 for _ in range(3)]
    gf = [[None] * 4 for _ in range(3)]
    twins = []

    def line(p, ref, jb, jc):
        return ref.at[place(p, ALL, net.along(ORDER[p][1], jb), net.along(ORDER[p][2], jc))]

    def to_twin(p, jb, jc):
        made = go(line(p, x[p], jb, jc), line(p, t[p], jb, jc), net.twin())
        twins.append((p, jb, jc, made))

    def spread(p, n):
        src = line(p, x[p], JS[n], 0)
        gc[p][n] = [go(src, src, net.near(ORDER[p][2], k)) for k in (1, 3)]
        to_twin(p, JS[n], 0)

    def multiply(p, ref, jc, half):
        off, width = PARTS[p]
        where = place(p, ALL, ALL, net.along(ORDER[p][2], jc))

        def step(k, carry):
            lanes = pl.ds(pl.multiple_of(k * TILE, TILE), TILE)
            rows = pl.ds(pl.multiple_of(off + k * TILE, TILE), TILE)
            left = ref[where + (ALL, lanes)].reshape(256, TILE)
            accg[where] += jnp.dot(left, wg[half, rows, :], preferred_element_type=jnp.float32).reshape(4, 4, 16, 256)
            accu[where] += jnp.dot(left, wu[half, rows, :], preferred_element_type=jnp.float32).reshape(4, 4, 16, 256)
            return carry

        lax.fori_loop(0, width // TILE, step, 0)

    for p in range(3):
        for made in ga[p]:
            made.wait_recv()
        src = line(p, x[p], 0, 0)
        gb[p] = [go(src, src, net.near(ORDER[p][1], k)) for k in (1, 3, 2)]
        spread(p, 0)
    for made in loads:
        made.wait()
    for n in (1, 2, 3):
        for p in range(3):
            gb[p][SLOT[JS[n]]].wait_recv()
            spread(p, n)
    for n in range(4):
        for p in range(3):
            gc[p][n][0].wait_recv()
            gc[p][n][1].wait_recv()
            if n % 2 == 0:
                src = line(p, x[p], JS[n], 3)
                gf[p][n] = go(src, src, net.near(ORDER[p][2], 1))
            else:
                src = line(p, x[p], JS[n], 1)
                gf[p][n] = go(src, src, net.near(ORDER[p][2], 3))
            to_twin(p, JS[n], 3)
            to_twin(p, JS[n], 1)
            if n == 0:
                multiply(p, x[p], 0, 0)
            if n == 1:
                for q, jb, jc, made in twins:
                    if q == p and jc == 0:
                        made.wait_recv()
                multiply(p, t[p], 0, 1)
    for p in range(3):
        multiply(p, x[p], 1, 0)
        multiply(p, x[p], 3, 0)
        for jc in (1, 3):
            for q, jb, kc, made in twins:
                if q == p and kc == jc:
                    made.wait_recv()
            multiply(p, t[p], jc, 1)
    for p in range(3):
        for n in range(4):
            gf[p][n].wait_recv()
            to_twin(p, JS[n], 2)
        multiply(p, x[p], 2, 0)
    for p in range(3):
        for q, jb, kc, made in twins:
            if q == p and kc == 2:
                made.wait_recv()
        multiply(p, t[p], 2, 1)
    for made in sent:
        made.wait_send()
    sent.clear()

    rank = lax.axis_index("dp")
    mine = jnp.logical_or(lane == rank, lane == rank + 32)

    def activate(k, carry):
        g = accg[k].reshape(256, 256)
        u = accu[k].reshape(256, 256)
        c = x[2][k, :, :, :, 1024:1152].reshape(256, 128).astype(jnp.float32)
        c = jnp.sum(jnp.where(mine, c, 0.0), axis=1, keepdims=True)
        hid[k] = (g * jax.nn.sigmoid(g) * u * c).astype(jnp.bfloat16).reshape(4, 4, 16, 256)
        return carry

    lax.fori_loop(0, 4, activate, 0)

    def down_twin(p, jc):
        off, width = PARTS[p]
        where = place(p, ALL, ALL, net.along(ORDER[p][2], jc))

        def step(k, carry):
            lanes = pl.ds(pl.multiple_of(k * TILE, TILE), TILE)
            cols = pl.ds(pl.multiple_of(off + k * TILE, TILE), TILE)
            got = jnp.dot(hid[where].reshape(256, 256), wd[1, :, cols], preferred_element_type=jnp.float32)
            t[p][where + (ALL, lanes)] = got.astype(jnp.bfloat16).reshape(4, 4, 16, TILE)
            return carry

        lax.fori_loop(0, width // TILE, step, 0)
        return go(t[p].at[where + (ALL, pl.ds(0, width))], r[p].at[where], net.twin())

    def down_own(p, jc, made):
        off, width = PARTS[p]
        where = place(p, ALL, ALL, net.along(ORDER[p][2], jc))
        made.wait_recv()

        def step(k, carry):
            lanes = pl.ds(pl.multiple_of(k * TILE, TILE), TILE)
            cols = pl.ds(pl.multiple_of(off + k * TILE, TILE), TILE)
            got = jnp.dot(hid[where].reshape(256, 256), wd[0, :, cols], preferred_element_type=jnp.float32)
            got = got + r[p][where + (ALL, lanes)].reshape(256, TILE).astype(jnp.float32)
            x[p][where + (ALL, lanes)] = got.astype(jnp.bfloat16).reshape(4, 4, 16, TILE)
            return carry

        lax.fori_loop(0, width // TILE, step, 0)

    JB = (2, 1, 3, 0)
    PLUS, MINUS = (0, 3), (1, 2)
    steps = [(p, jc) for jc in (2, 1, 3, 0) for p in range(3)]
    made_twin = {}
    h1, h2 = {}, {}

    def add_line(p, jb, jc, others):
        b, c = net.along(ORDER[p][1], jb), net.along(ORDER[p][2], jc)

        def step(k, carry):
            where = place(p, k, b, c) + (ALL, pl.ds(0, PARTS[p][1]))
            total = x[p][where].astype(jnp.float32)
            for ref, index in others:
                total = total + ref[index + (k,)].astype(jnp.float32)
            x[p][where] = total.astype(jnp.bfloat16)
            return carry

        lax.fori_loop(0, 4, step, 0)

    def out_line(p, jb, jc):
        where = place(p, ALL, net.along(ORDER[p][1], jb), net.along(ORDER[p][2], jc))
        return x[p].at[where + (ALL, pl.ds(0, PARTS[p][1]))]

    def send_c1(p):
        h1[p] = []
        for i, n in enumerate(PLUS):
            h1[p].append(go(out_line(p, JB[n], 2), ca[p].at[0, i], net.near(ORDER[p][2], 1)))
        for i, n in enumerate(MINUS):
            h1[p].append(go(out_line(p, JB[n], 2), ca[p].at[1, i], net.near(ORDER[p][2], 3)))

    def send_c2(p, jc):
        way = 0 if jc == 1 else 1
        mine = PLUS if jc == 1 else MINUS
        for i in range(2):
            h1[p][way * 2 + i].wait_recv()
        for n in range(4):
            if n in mine:
                add_line(p, JB[n], jc, [(ca[p], (way, mine.index(n)))])
            h2[p, way, n] = go(out_line(p, JB[n], jc), cb[p].at[way, n], net.near(ORDER[p][2], jc))

    made_twin[steps[0]] = down_twin(*steps[0])
    for i, (p, jc) in enumerate(steps):
        if i + 1 < len(steps):
            made_twin[steps[i + 1]] = down_twin(*steps[i + 1])
        down_own(p, jc, made_twin[p, jc])
        if jc == 2:
            send_c1(p)
        elif jc != 0:
            send_c2(p, jc)
    hb = [[None] * 4 for _ in range(3)]
    for n in range(3):
        for p in range(3):
            for way in range(2):
                h2[p, way, n].wait_recv()
            add_line(p, JB[n], 0, [(cb[p], (0, n)), (cb[p], (1, n))])
            hb[p][n] = go(out_line(p, JB[n], 0), bb[p].at[n], net.near(ORDER[p][1], JB[n]))
    for p in range(3):
        for way in range(2):
            h2[p, way, 3].wait_recv()
        for n in range(3):
            hb[p][n].wait_recv()
        add_line(p, 0, 0, [(cb[p], (0, 3)), (cb[p], (1, 3))] + [(bb[p], (n,)) for n in range(3)])
    haa = []
    for p in range(3):
        _, mb, mc = (net.pos[axis] for axis in ORDER[p])
        for n, k in enumerate((2, 1, 3)):
            src = x[p].at[place(p, net.along(ORDER[p][0], k), mb, mc) + (ALL, pl.ds(0, PARTS[p][1]))]
            haa.append(go(src, aa[p].at[n], net.near(ORDER[p][0], k)))
    for p, (off, width) in enumerate(PARTS):
        for n in range(3):
            haa[p * 3 + n].wait_recv()
        total = x[p][px, py, pz, :, 0:width].astype(jnp.float32)
        for n in range(3):
            total = total + aa[p][n].astype(jnp.float32)
        fin[0, :, off:off + width] = s16[:, off:off + width] + total
    theirs = fin.at[0, pl.ds(pl.multiple_of((1 - core) * 8, 8), 8)]
    last = net.copy(theirs, fin.at[1, pl.ds(0, 8)], net.twin())
    mine = fin[0, pl.ds(pl.multiple_of(core * 8, 8), 8)]
    out[:, pl.ds(pl.multiple_of(core * HALF, HALF), HALF)] = mine.astype(jnp.bfloat16)
    last.wait_recv()
    out[:, pl.ds(pl.multiple_of((1 - core) * HALF, HALF), HALF)] = fin[1, 0:8].astype(jnp.bfloat16)
    last.wait_send()
    for made in sent:
        made.wait_send()


def experts(s16, gain, ids, gates, owner, w_gate, w_up, w_down):
    bf = jnp.bfloat16
    slots = 180
    vm = pl.BlockSpec(memory_space=pltpu.VMEM)
    hbm = pl.BlockSpec(memory_space=pl.ANY)
    grid = [pltpu.VMEM((4, 4, 4, 16, w), bf) for w in GRIDS]
    return pl.pallas_call(
        expert_kernel,
        out_shape=jax.ShapeDtypeStruct((8, WIDE), bf),
        in_specs=[vm, vm, vm, vm, pl.BlockSpec(memory_space=pltpu.SMEM), hbm, hbm, hbm],
        out_specs=vm,
        scratch_shapes=grid + grid + [
            pltpu.VMEM((2, HALF, 256), bf),
            pltpu.VMEM((2, HALF, 256), bf),
            pltpu.VMEM((2, 256, HALF), bf),
            pltpu.VMEM((4, 4, 4, 16, 256), jnp.float32),
            pltpu.VMEM((4, 4, 4, 16, 256), jnp.float32),
            pltpu.VMEM((4, 4, 4, 16, 256), bf),
        ] + [pltpu.VMEM((4, 4, 4, 16, w), bf) for _, w in PARTS]
        + [pltpu.VMEM((2, 2, 4, 16, w), bf) for _, w in PARTS]
        + [pltpu.VMEM((2, 4, 4, 16, w), bf) for _, w in PARTS]
        + [pltpu.VMEM((3, 4, 16, w), bf) for _, w in PARTS]
        + [pltpu.VMEM((3, 16, w), bf) for _, w in PARTS]
        + [
            pltpu.VMEM((2, 24, 128), jnp.float32),
            pltpu.VMEM((16, 128), jnp.float32),
            pltpu.VMEM((2, 16, HALF), jnp.float32),
            pltpu.SemaphoreType.DMA((6,)),
            pltpu.SemaphoreType.DMA((slots,)),
            pltpu.SemaphoreType.DMA((slots,)),
        ],
        compiler_params=pltpu.CompilerParams(collective_id=2, has_side_effects=True, vmem_limit_bytes=62 * 2**20),
        name="experts",
    )(s16, gain.reshape(2, 1, HALF), ids, gates, owner, w_gate, w_up, w_down)


softmax_scale = 192.0 ** (-0.5)
OWN = 224
WITHIN = (((0,), (0,)), ((), ()))
LAST = (((1,), (1,)), ((), ()))
MIG = ((0, 32, 1, 2), (32, 48, 2, 1))


def attend_kernel(
    query, pool, table, scales, lens_s, mig_s, value_up, out_w, residual,
    s16, blocks_out, scales_out,
    kt, kp, hot, vu, wt, lat, h00, h01, h10, h11, n00, n01, n10, n11, part, px, rx, sp, gx, res, mg, quarter, lane_scale, row,
    load, send, recv, recv2, send2,
):
    net = Links(send, recv)
    core = net.core
    x, y, z = net.pos
    rank = (y * 4 + z) * 2 + core
    heads = ((h00, h01), (h10, h11))
    twin_heads = ((n00, n01), (n10, n11))
    f32, bf = jnp.float32, jnp.bfloat16

    loads = []
    for i in range(8):
        made = pltpu.make_async_copy(pool.at[pl.ds(i * 8, 8)], kt.at[pl.ds(i * 8, 8)], load.at[i])
        made.start()
        loads.append(made)
    late = []
    for i, (src, dst) in enumerate(((value_up, vu), (out_w, wt.at[pl.ds(0, OWN)]))):
        made = pltpu.make_async_copy(src, dst, load.at[8 + i])
        made.start()
        late.append(made)

    barrier = pltpu.get_barrier_semaphore()
    for k in range(1, 32):
        other = lax.rem(rank + k, 32)
        pl.semaphore_signal(barrier, inc=1, device_id=(other, x), device_id_type=MESH)
    for k in range(1, 4):
        pl.semaphore_signal(barrier, inc=1, device_id=net.near(0, k), device_id_type=MESH)

    rows = lax.broadcasted_iota(jnp.int32, (32, 128), 0)
    widen = (rows == lax.broadcasted_iota(jnp.int32, (32, 128), 1) // 4).astype(f32)
    names = jnp.dot(table[...].astype(f32), widen, preferred_element_type=f32)
    held = lax.broadcasted_iota(jnp.int32, (4, 128), 0) == lax.rem(lax.broadcasted_iota(jnp.int32, (4, 128), 1), 4)
    names = jnp.sum(jnp.where(held, names, 0.0), axis=0, keepdims=True)
    names = jnp.broadcast_to(names, (128, 128))
    turned = (names == lax.broadcasted_iota(jnp.int32, (128, 128), 0).astype(f32)).astype(f32)
    hot[0:128] = turned.T.astype(bf)
    leaving, sender, has_in = 0, 0, 0
    for i in range(16):
        goes = mig_s[1, i] == rank
        leaving += jnp.where(goes, mig_s[0, i] - rank * 32, 0)
        comes = mig_s[2, i] == rank
        sender += jnp.where(comes, mig_s[1, i], 0)
        has_in += jnp.where(comes, 1, 0)
    slot = leaving * 4 + x
    only = lax.broadcasted_iota(jnp.int32, (128, 128), 0) == slot
    only = jnp.sum(jnp.where(only, hot[0:128].astype(f32), 0.0), axis=0, keepdims=True)
    hot[128:144] = jnp.broadcast_to(only, (16, 128)).astype(bf)
    slot_scale = jnp.dot(jnp.broadcast_to(scales[...].astype(f32), (16, 128)).astype(bf), turned.astype(bf), preferred_element_type=f32)[0:8]
    groups = lax.broadcasted_iota(jnp.int32, (8, 128), 0) == lax.broadcasted_iota(jnp.int32, (8, 128), 1) // 16
    spread = (
        lax.rem(lax.broadcasted_iota(jnp.int32, (128, 1024), 0), 16)
        == lax.rem(lax.broadcasted_iota(jnp.int32, (128, 1024), 1), 16)
    ).astype(bf)
    lane_scale[...] = jnp.dot(jnp.where(groups, slot_scale, 0.0).astype(bf), spread, preferred_element_type=f32).reshape(8, 1, 1024)
    wt[pl.ds(OWN, 32)] = jnp.zeros((32, 2048), bf)

    for i in range(8):
        loads[i].wait()

        def turn(k, carry):
            for n in range(2):
                at = i * 8 + k * 2 + n
                got = lax.dot_general(hot[...], kt[at], LAST, preferred_element_type=f32)
                kp[at] = got[0:128].astype(bf)
                row[pl.ds(at, 1)] = got[128:129]
            return carry

        lax.fori_loop(0, 4, turn, 0)

    its = jnp.sum(jnp.where(lax.broadcasted_iota(jnp.int32, (8, 128), 1) == slot, slot_scale, 0.0)[0:1], axis=1, keepdims=True)
    mg[core, y, z, 0:64] = row[...].astype(bf)
    mg[core, y, z, 64:80] = jnp.broadcast_to(its, (16, 576)).astype(bf)

    pl.semaphore_wait(barrier, 34)
    sent = []

    def go(src, dst, device):
        made = net.copy(src, dst, device)
        sent.append(made)
        return made

    mine = residual[:, pl.ds(pl.multiple_of(core * HALF, HALF), HALF)].astype(f32)
    rows = pl.ds(pl.multiple_of(core * 8, 8), 8)
    res[0, rows] = mine
    res[1, rows] = residual[:, pl.ds(pl.multiple_of((1 - core) * HALF, HALF), HALF)].astype(f32)
    swap = go(res.at[1, rows], res.at[0, rows], net.twin())

    def mig_line(i, first):
        off, n, a, b = MIG[i]
        r = pl.ds(off, n)
        return mg.at[core, first, :, r] if a == 2 else mg.at[core, :, first, r]

    m1 = []
    for off, n, a, b in MIG:
        src = mg.at[core, y, z, pl.ds(off, n)]
        m1.append([go(src, src, net.near(a, k)) for k in (1, 3, 2)])
    m2, mt = [None, None], []

    def mig_spread(i):
        off, n, a, b = MIG[i]
        for made in m1[i]:
            made.wait_recv()
        src = mig_line(i, net.pos[b])
        m2[i] = [go(src, src, net.near(b, k)) for k in (1, 3, 2)]
        mt.append(go(src, src, net.twin()))

    def mig_twin(i):
        b = MIG[i][3]
        for k, made in zip((1, 3, 2), m2[i]):
            made.wait_recv()
            src = mig_line(i, net.along(b, 4 - k))
            mt.append(go(src, src, net.twin()))

    def attend(g, carry):
        q = query[pl.ds(g * 4, 4)].reshape(64, 576)
        keys = kp[:, pl.ds(pl.multiple_of(g * 16, 16), 16), :].reshape(1024, 576)
        scale = lane_scale[g]
        score = lax.dot_general(q, keys, LAST, preferred_element_type=f32)
        lane = lax.broadcasted_iota(jnp.int32, (1, 1024), 1)
        which = lax.rem(lane, 16)
        owner = which // 4
        place_ = lax.rem(which, 4) * 64 + lane // 16
        limit = jnp.where(owner == 0, lens_s[g * 4], jnp.where(owner == 1, lens_s[g * 4 + 1], jnp.where(owner == 2, lens_s[g * 4 + 2], lens_s[g * 4 + 3])))
        holder = jnp.where(place_ < limit, owner, -1)
        live = holder == lax.broadcasted_iota(jnp.int32, (64, 1024), 0) // 16
        score = jnp.where(live, score * (scale * softmax_scale), -1e30)
        top = jnp.max(score, axis=1, keepdims=True)
        expo = jnp.exp(score - top)
        total = jnp.sum(expo, axis=1, keepdims=True)
        coef = (expo * (1.0 / total) * scale).astype(bf)
        got = jnp.dot(coef, keys[:, 0:512], preferred_element_type=f32)
        for n in range(4):
            lat[n, pl.ds(pl.multiple_of(g * 64, 64), 64)] = got[:, n * 128:(n + 1) * 128]
        return carry

    ga = [[None] * 2, [None] * 2]
    gb = [[None] * 2, [None] * 2]
    tw = [[[], []], [[], []]]
    AXES = ((1, 2), (2, 1))

    def value_map(half):
        for h in range(16):
            rows = [lat[n, pl.ds(half * 256 + h, 16, stride=16), :] for n in range(4)]
            rows = jnp.concatenate(rows, axis=1).astype(bf)
            got = jnp.dot(rows, vu[h], preferred_element_type=f32).astype(bf)
            heads[half][h // 8][y, z, :, (h % 8) * 128:(h % 8 + 1) * 128] = got

    def head_line(ref, p, first):
        return ref.at[first] if p == 0 and False else (ref.at[:, first] if AXES[p][0] == 1 else ref.at[first])

    def head_start(half):
        for p in range(2):
            src = heads[half][p].at[y, z]
            ga[half][p] = [go(src, src, net.near(AXES[p][0], k)) for k in (1, 3, 2)]

    def head_twin(half, p, first):
        tw[half][p].append(go(head_line(heads[half][p], p, first), head_line(twin_heads[half][p], p, first), net.twin()))

    def head_spread(half):
        for p in range(2):
            for made in ga[half][p]:
                made.wait_recv()
            first = net.pos[AXES[p][1]]
            src = head_line(heads[half][p], p, first)
            gb[half][p] = [go(src, src, net.near(AXES[p][1], k)) for k in (1, 3, 2)]
            head_twin(half, p, first)

    def head_finish(half):
        for i in range(3):
            for p in range(2):
                gb[half][p][i].wait_recv()
                head_twin(half, p, net.along(AXES[p][1], 4 - (1, 3, 2)[i]))

    def project(half, refs, who):
        def step(k, carry):
            total = lax.dot_general(refs[0][k].reshape(64, 1024), wt[:, 0:1024], LAST, preferred_element_type=f32)
            total += lax.dot_general(refs[1][k].reshape(64, 1024), wt[:, 1024:2048], LAST, preferred_element_type=f32)
            part[half, who, k] = total.reshape(4, 16, 256)
            return carry

        lax.fori_loop(0, 4, step, 0)

    lax.fori_loop(0, 2, attend, 0)
    mig_spread(0)
    mig_spread(1)
    lax.fori_loop(2, 4, attend, 0)
    for made in late:
        made.wait()
    value_map(0)
    head_start(0)
    lax.fori_loop(4, 6, attend, 0)
    head_spread(0)
    lax.fori_loop(6, 8, attend, 0)
    value_map(1)
    head_start(1)
    mig_twin(0)
    mig_twin(1)
    for made in mt:
        made.wait_recv()
    found = mg[lax.rem(sender, 2), sender // 8, lax.rem(sender // 2, 4)]
    quarter[x] = jnp.where(has_in > 0, found, jnp.zeros_like(found))
    mx = [go(quarter.at[x], quarter.at[x], net.near(0, k)) for k in (1, 3, 2)]
    head_spread(1)
    head_finish(0)
    project(0, heads[0], core)
    for p in range(2):
        for made in tw[0][p]:
            made.wait_recv()
    project(0, twin_heads[0], 1 - core)

    def shares(half):
        for n in range(2):
            rows = pl.ds(n * 8, 8)
            both = jnp.concatenate([part[half, 0, :, :, rows], part[half, 1, :, :, rows]], axis=2)
            px[half * 2 + n] = both.astype(bf)

    shares(0)
    head_finish(1)
    project(1, heads[1], core)
    for p in range(2):
        for made in tw[1][p]:
            made.wait_recv()
    project(1, twin_heads[1], 1 - core)
    shares(1)
    back = [go(px.at[net.along(0, k)], rx.at[n], net.near(0, k)) for n, k in enumerate((1, 3, 2))]
    for made in mx:
        made.wait_recv()
    for i in range(4):
        blocks_out[i] = quarter[i, 0:64]
        scales_out[i] = quarter[i, 64:80, 0:128]
    for made in back:
        made.wait_recv()

    def add(k, carry):
        total = px[x, k].astype(f32)
        for n in range(3):
            total = total + rx[n, k].astype(f32)
        sp[k] = total.astype(bf)
        return carry

    lax.fori_loop(0, 4, add, 0)
    to_core = y // 2
    here = (lax.rem(y, 2) * 4 + z) * 2 + core
    away = []
    for k in range(16):
        ty, tz = net.along(1, k // 4), net.along(2, k % 4)
        made = pltpu.make_async_remote_copy(
            src_ref=sp.at[ty, tz], dst_ref=gx.at[here], send_sem=send2.at[k], recv_sem=recv2.at[here],
            device_id=net.device((x, ty, tz), to_core), device_id_type=MESH,
        )
        away.append(made)
        if k:
            made.start()

    @pl.when(to_core != core)
    def _():
        away[0].start()

    @pl.when(to_core == core)
    def _():
        gx[here] = sp[y, z]

    swap.wait_recv()
    for j in range(16):
        made = pltpu.make_async_remote_copy(
            src_ref=sp.at[0, 0], dst_ref=gx.at[j], send_sem=send2.at[j], recv_sem=recv2.at[j],
            device_id=net.twin(), device_id_type=MESH,
        )

        @pl.when(jnp.logical_or(to_core != core, here != j))
        def _():
            made.wait_recv()

        cols = slice(j * OWN, (j + 1) * OWN)
        s16[:, cols] = res[0, :, cols] + gx[j].astype(f32)[:, 0:OWN]
    for k in range(1, 16):
        away[k].wait_send()

    @pl.when(to_core != core)
    def _():
        away[0].wait_send()

    for made in sent:
        made.wait_send()


def attend_all(query, pool, block_scale, table, lengths, migration, value_up, out_weight, residual):
    bf, f32 = jnp.bfloat16, jnp.float32
    vm = pl.BlockSpec(memory_space=pltpu.VMEM)
    sm = pl.BlockSpec(memory_space=pltpu.SMEM)
    hbm = pl.BlockSpec(memory_space=pl.ANY)
    head = [pltpu.VMEM((4, 4, 16, 1024), bf)] * 8
    return pl.pallas_call(
        attend_kernel,
        out_shape=(
            jax.ShapeDtypeStruct((16, HALF), f32),
            jax.ShapeDtypeStruct((4, 64, 576), bf),
            jax.ShapeDtypeStruct((4, 16, 128), bf),
        ),
        in_specs=[vm, hbm, vm, vm, sm, sm, hbm, hbm, vm],
        out_specs=(vm, vm, vm),
        scratch_shapes=[
            pltpu.VMEM((64, 576, 128), bf),
            pltpu.VMEM((64, 128, 576), bf),
            pltpu.VMEM((144, 128), bf),
            pltpu.VMEM((16, 512, 128), bf),
            pltpu.VMEM((256, 2048), bf),
            pltpu.VMEM((4, 512, 128), f32),
        ] + head + [
            pltpu.VMEM((2, 2, 4, 4, 16, 256), f32),
            pltpu.VMEM((4, 4, 4, 16, 256), bf),
            pltpu.VMEM((3, 4, 4, 16, 256), bf),
            pltpu.VMEM((4, 4, 16, 256), bf),
            pltpu.VMEM((16, 16, 256), bf),
            pltpu.VMEM((2, 16, HALF), f32),
            pltpu.VMEM((2, 4, 4, 80, 576), bf),
            pltpu.VMEM((4, 80, 576), bf),
            pltpu.VMEM((8, 1, 1024), f32),
            pltpu.VMEM((64, 576), f32),
            pltpu.SemaphoreType.DMA((10,)),
            pltpu.SemaphoreType.DMA((90,)),
            pltpu.SemaphoreType.DMA((90,)),
            pltpu.SemaphoreType.DMA((16,)),
            pltpu.SemaphoreType.DMA((16,)),
        ],
        compiler_params=pltpu.CompilerParams(collective_id=1, has_side_effects=True, vmem_limit_bytes=62 * 2**20),
        name="attend",
    )(
        query, jnp.transpose(pool, (1, 2, 0)), table.T, block_scale.reshape(1, 128), lengths,
        migration.T, value_up, out_weight.T, residual,
    )


def body(
    query, cache_pool, block_scale, block_table, lengths, migration, value_up, out_weight, residual, norm_gain,
    expert_ids, gate_weights, expert_owner, w_gate, w_up, w_down,
):
    s16, blocks, scales = attend_all(
        query, cache_pool, block_scale, block_table, lengths, migration, value_up, out_weight, residual
    )
    mixed = experts(s16, norm_gain, expert_ids, gate_weights, expert_owner, w_gate, w_up, w_down)
    return (mixed, blocks[None], scales[:, 0, 0][None])


def solution(mesh):
    return jax.shard_map(
        body,
        mesh=mesh,
        in_specs=(
            P("dp", "tp", None),
            P("dp", None, None),
            P("dp"),
            P("dp", None),
            P("dp"),
            P(),
            P("tp", None, None),
            P("tp", "dp"),
            P(("dp", "tp"), None),
            P(),
            P(("dp", "tp"), None),
            P(("dp", "tp"), None),
            P(),
            P("dp", None, "tp"),
            P("dp", None, "tp"),
            P("dp", "tp", None),
        ),
        out_specs=(P(("dp", "tp"), None), P("dp", None, None, None), P("dp", None)),
        check_vma=False,
    )
```

```python
import functools
import jax
import jax.numpy as jnp
from jax import lax
from jax.experimental import pallas as pl
from jax.experimental.pallas import tpu as pltpu
from jax.sharding import PartitionSpec as P

MESH = pl.DeviceIdType.MESH
norm_eps = 1e-06
WIDE = 7168
HALF = 3584
PARTS = ((0, 1280), (1280, 1280), (2560, 1024))
GRIDS = (1280, 1280, 1152)
ORDER = ((0, 1, 2), (1, 2, 0), (2, 0, 1))
TILE = 256


class Links:
    def __init__(self, send, recv):
        self.send, self.recv, self.used = send, recv, 0
        rank = lax.axis_index("dp")
        self.core = lax.rem(rank, 2)
        self.pos = (lax.axis_index("tp"), rank // 8, lax.rem(rank // 2, 4))

    def device(self, pos, core):
        return ((pos[1] * 4 + pos[2]) * 2 + core, pos[0])

    def along(self, axis, step):
        return lax.rem(self.pos[axis] + step, 4)

    def near(self, axis, step):
        pos = list(self.pos)
        pos[axis] = self.along(axis, step)
        return self.device(pos, self.core)

    def twin(self):
        return self.device(self.pos, 1 - self.core)

    def copy(self, src, dst, device):
        slot = self.used
        self.used += 1
        made = pltpu.make_async_remote_copy(
            src_ref=src,
            dst_ref=dst,
            send_sem=self.send.at[slot],
            recv_sem=self.recv.at[slot],
            device_id=device,
            device_id_type=MESH,
        )
        made.start()
        return made


def place(part, a, b, c):
    index = [None, None, None]
    for axis, value in zip(ORDER[part], (a, b, c)):
        index[axis] = value
    return tuple(index)


ALL = slice(None)


softmax_scale = 192.0 ** (-0.5)
OWN = 224
WITHIN = (((0,), (0,)), ((), ()))
LAST = (((1,), (1,)), ((), ()))
MIG = ((0, 32, 1, 2), (32, 48, 2, 1))


def kernel(
    query, pool, table, scales, lens_s, mig_s, value_up, out_w, residual,
    gain, ids, gates, owner, wg_in, wu_in, wd_in,
    out, blocks_out, scales_out,
    x0, x1, x2, t0, t1, t2, wg, wu, wd, accg, accu, hid,
    r0, r1, r2, ca0, ca1, ca2, cb0, cb1, cb2, bb0, bb1, bb2, aa0, aa1, aa2,
    sums, both, fin,
    kt, hot, vu, wt, lat, h00, h01, h10, h11, n00, n01, n10, n11, part, px_, rx, sp, gx, res, mg, quarter, lane_scale, row, s16,
    load, send, recv, recv2, send2,
):
    keys_in = (t0, t1, r0, r1)
    net = Links(send, recv)
    core = net.core
    x, y, z = net.pos
    rank = (y * 4 + z) * 2 + core
    heads = ((h00, h01), (h10, h11))
    twin_heads = ((n00, n01), (n10, n11))
    f32, bf = jnp.float32, jnp.bfloat16

    def fetch(i, slot):
        return pltpu.make_async_copy(pool.at[pl.ds(i * 4, 4)], kt.at[slot], load.at[slot])

    for i in range(4):
        fetch(i, i).start()
    late = []
    for i, (src, dst) in enumerate(((value_up, vu), (out_w, wt.at[pl.ds(0, OWN)]))):
        made = pltpu.make_async_copy(src, dst, load.at[4 + i])
        made.start()
        late.append(made)

    barrier = pltpu.get_barrier_semaphore()
    for k in range(1, 32):
        other = lax.rem(rank + k, 32)
        pl.semaphore_signal(barrier, inc=1, device_id=(other, x), device_id_type=MESH)
    for k in range(1, 4):
        pl.semaphore_signal(barrier, inc=1, device_id=net.near(0, k), device_id_type=MESH)

    rows = lax.broadcasted_iota(jnp.int32, (32, 128), 0)
    widen = (rows == lax.broadcasted_iota(jnp.int32, (32, 128), 1) // 4).astype(f32)
    names = jnp.dot(table[...].astype(f32), widen, preferred_element_type=f32)
    held = lax.broadcasted_iota(jnp.int32, (4, 128), 0) == lax.rem(lax.broadcasted_iota(jnp.int32, (4, 128), 1), 4)
    names = jnp.sum(jnp.where(held, names, 0.0), axis=0, keepdims=True)
    names = jnp.broadcast_to(names, (128, 128))
    turned = (names == lax.broadcasted_iota(jnp.int32, (128, 128), 0).astype(f32)).astype(f32)
    hot[0:128] = turned.T.astype(bf)
    leaving, sender, has_in = 0, 0, 0
    for i in range(16):
        goes = mig_s[1, i] == rank
        leaving += jnp.where(goes, mig_s[0, i] - rank * 32, 0)
        comes = mig_s[2, i] == rank
        sender += jnp.where(comes, mig_s[1, i], 0)
        has_in += jnp.where(comes, 1, 0)
    slot = leaving * 4 + x
    only = lax.broadcasted_iota(jnp.int32, (128, 128), 0) == slot
    only = jnp.sum(jnp.where(only, hot[0:128].astype(f32), 0.0), axis=0, keepdims=True)
    hot[128:144] = jnp.broadcast_to(only, (16, 128)).astype(bf)
    slot_scale = jnp.dot(jnp.broadcast_to(scales[...].astype(f32), (16, 128)).astype(bf), turned.astype(bf), preferred_element_type=f32)[0:8]
    groups = lax.broadcasted_iota(jnp.int32, (8, 128), 0) == lax.broadcasted_iota(jnp.int32, (8, 128), 1) // 16
    spread = (
        lax.rem(lax.broadcasted_iota(jnp.int32, (128, 1024), 0), 16)
        == lax.rem(lax.broadcasted_iota(jnp.int32, (128, 1024), 1), 16)
    ).astype(bf)
    lane_scale[...] = jnp.dot(jnp.where(groups, slot_scale, 0.0).astype(bf), spread, preferred_element_type=f32).reshape(8, 1, 1024)
    wt[pl.ds(OWN, 32)] = jnp.zeros((32, 2048), bf)

    def turn(i, carry):
        slot = lax.rem(i, 4)
        fetch(i, slot).wait()
        for n in range(4):
            got = lax.dot_general(hot[...], kt[slot, n], LAST, preferred_element_type=f32)
            for g in range(8):
                keys_in[g // 2][i // 4, lax.rem(i, 4), n, :, (g % 2) * 640:(g % 2) * 640 + 576] = got[g * 16:(g + 1) * 16].astype(bf)
            row[pl.ds(i * 4 + n, 1)] = got[128:129]

        @pl.when(i < 12)
        def _():
            fetch(i + 4, slot).start()

        return carry

    lax.fori_loop(0, 16, turn, 0)
    loads = []
    for half in range(2):
        which = core if half == 0 else 1 - core
        rows = pl.ds(pl.multiple_of(which * HALF, HALF), HALF)
        for n, (src, dst) in enumerate(
            ((wg_in.at[0, rows, :], wg.at[half]), (wu_in.at[0, rows, :], wu.at[half]), (wd_in.at[0, :, rows], wd.at[half]))
        ):
            made = pltpu.make_async_copy(src, dst, load.at[6 + half * 3 + n])
            made.start()
            loads.append(made)

    its = jnp.sum(jnp.where(lax.broadcasted_iota(jnp.int32, (8, 128), 1) == slot, slot_scale, 0.0)[0:1], axis=1, keepdims=True)
    mg[core, y, z, 0:64] = row[...].astype(bf)
    mg[core, y, z, 64:80] = jnp.broadcast_to(its, (16, 576)).astype(bf)

    pl.semaphore_wait(barrier, 34)
    sent = []

    def go(src, dst, device):
        made = net.copy(src, dst, device)
        sent.append(made)
        return made

    mine = residual[:, pl.ds(pl.multiple_of(core * HALF, HALF), HALF)].astype(f32)
    rows = pl.ds(pl.multiple_of(core * 8, 8), 8)
    res[0, rows] = mine
    res[1, rows] = residual[:, pl.ds(pl.multiple_of((1 - core) * HALF, HALF), HALF)].astype(f32)
    swap = go(res.at[1, rows], res.at[0, rows], net.twin())

    def mig_line(i, first):
        off, n, a, b = MIG[i]
        r = pl.ds(off, n)
        return mg.at[core, first, :, r] if a == 2 else mg.at[core, :, first, r]

    m1 = []
    for off, n, a, b in MIG:
        src = mg.at[core, y, z, pl.ds(off, n)]
        m1.append([go(src, src, net.near(a, k)) for k in (1, 3, 2)])
    m2, mt = [None, None], []

    def mig_spread(i):
        off, n, a, b = MIG[i]
        for made in m1[i]:
            made.wait_recv()
        src = mig_line(i, net.pos[b])
        m2[i] = [go(src, src, net.near(b, k)) for k in (1, 3, 2)]
        mt.append(go(src, src, net.twin()))

    def mig_twin(i):
        b = MIG[i][3]
        for k, made in zip((1, 3, 2), m2[i]):
            made.wait_recv()
            src = mig_line(i, net.along(b, 4 - k))
            mt.append(go(src, src, net.twin()))

    def attend(b, k, carry):
        g = b * 2 + k
        q = query[pl.ds(g * 4, 4)].reshape(64, 576)
        keys = keys_in[b][:, :, :, :, pl.ds(pl.multiple_of(k * 640, 640), 576)].reshape(1024, 576)
        scale = lane_scale[g]
        score = lax.dot_general(q, keys, LAST, preferred_element_type=f32)
        lane = lax.broadcasted_iota(jnp.int32, (1, 1024), 1)
        which = lax.rem(lane, 16)
        owner = which // 4
        place_ = lax.rem(which, 4) * 64 + lane // 16
        limit = jnp.where(owner == 0, lens_s[g * 4], jnp.where(owner == 1, lens_s[g * 4 + 1], jnp.where(owner == 2, lens_s[g * 4 + 2], lens_s[g * 4 + 3])))
        holder = jnp.where(place_ < limit, owner, -1)
        live = holder == lax.broadcasted_iota(jnp.int32, (64, 1024), 0) // 16
        score = jnp.where(live, score * (scale * softmax_scale), -1e30)
        top = jnp.max(score, axis=1, keepdims=True)
        expo = jnp.exp(score - top)
        total = jnp.sum(expo, axis=1, keepdims=True)
        coef = (expo * (1.0 / total) * scale).astype(bf)
        got = jnp.dot(coef, keys[:, 0:512], preferred_element_type=f32)
        for n in range(4):
            lat[n, pl.ds(pl.multiple_of(g * 64, 64), 64)] = got[:, n * 128:(n + 1) * 128]
        return carry

    ga = [[None] * 2, [None] * 2]
    gb = [[None] * 2, [None] * 2]
    tw = [[[], []], [[], []]]
    AXES = ((1, 2), (2, 1))

    def value_map(half):
        for h in range(16):
            rows = [lat[n, pl.ds(half * 256 + h, 16, stride=16), :] for n in range(4)]
            rows = jnp.concatenate(rows, axis=1).astype(bf)
            got = jnp.dot(rows, vu[h], preferred_element_type=f32).astype(bf)
            heads[half][h // 8][y, z, :, (h % 8) * 128:(h % 8 + 1) * 128] = got

    def head_line(ref, p, first):
        return ref.at[:, first] if p == 0 else ref.at[first]

    def head_start(half):
        for p in range(2):
            src = heads[half][p].at[y, z]
            ga[half][p] = [go(src, src, net.near(AXES[p][0], k)) for k in (1, 3, 2)]

    def head_twin(half, p, first):
        tw[half][p].append(go(head_line(heads[half][p], p, first), head_line(twin_heads[half][p], p, first), net.twin()))

    def head_spread(half):
        for p in range(2):
            for made in ga[half][p]:
                made.wait_recv()
            first = net.pos[AXES[p][1]]
            src = head_line(heads[half][p], p, first)
            gb[half][p] = [go(src, src, net.near(AXES[p][1], k)) for k in (1, 3, 2)]
            head_twin(half, p, first)

    def head_finish(half):
        for i in range(3):
            for p in range(2):
                gb[half][p][i].wait_recv()
                head_twin(half, p, net.along(AXES[p][1], 4 - (1, 3, 2)[i]))

    def project(half, refs, who):
        def step(k, carry):
            total = lax.dot_general(refs[0][k].reshape(64, 1024), wt[:, 0:1024], LAST, preferred_element_type=f32)
            total += lax.dot_general(refs[1][k].reshape(64, 1024), wt[:, 1024:2048], LAST, preferred_element_type=f32)
            part[half, who, k] = total.reshape(4, 16, 256)
            return carry

        lax.fori_loop(0, 4, step, 0)

    lax.fori_loop(0, 2, functools.partial(attend, 0), 0)
    lax.fori_loop(0, 2, functools.partial(attend, 1), 0)
    for made in late:
        made.wait()
    value_map(0)
    head_start(0)
    lax.fori_loop(0, 2, functools.partial(attend, 2), 0)
    head_spread(0)
    lax.fori_loop(0, 2, functools.partial(attend, 3), 0)
    value_map(1)
    head_start(1)
    head_spread(1)
    head_finish(0)
    project(0, heads[0], core)
    for p in range(2):
        for made in tw[0][p]:
            made.wait_recv()
    project(0, twin_heads[0], 1 - core)

    def shares(half):
        for n in range(2):
            rows = pl.ds(n * 8, 8)
            both = jnp.concatenate([part[half, 0, :, :, rows], part[half, 1, :, :, rows]], axis=2)
            px_[half * 2 + n] = both.astype(bf)

    shares(0)
    head_finish(1)
    project(1, heads[1], core)
    for p in range(2):
        for made in tw[1][p]:
            made.wait_recv()
    project(1, twin_heads[1], 1 - core)
    shares(1)
    back = [go(px_.at[net.along(0, k)], rx.at[n], net.near(0, k)) for n, k in enumerate((1, 3, 2))]
    mig_spread(0)
    mig_spread(1)
    for made in back:
        made.wait_recv()

    def add(k, carry):
        total = px_[x, k].astype(f32)
        for n in range(3):
            total = total + rx[n, k].astype(f32)
        sp[k] = total.astype(bf)
        return carry

    lax.fori_loop(0, 4, add, 0)
    to_core = y // 2
    here = (lax.rem(y, 2) * 4 + z) * 2 + core
    away = []
    for k in range(16):
        ty, tz = net.along(1, k // 4), net.along(2, k % 4)
        made = pltpu.make_async_remote_copy(
            src_ref=sp.at[ty, tz], dst_ref=gx.at[here], send_sem=send2.at[k], recv_sem=recv2.at[here],
            device_id=net.device((x, ty, tz), to_core), device_id_type=MESH,
        )
        away.append(made)
        if k:
            made.start()

    @pl.when(to_core != core)
    def _():
        away[0].start()

    @pl.when(to_core == core)
    def _():
        gx[here] = sp[y, z]

    swap.wait_recv()
    for j in range(16):
        made = pltpu.make_async_remote_copy(
            src_ref=sp.at[0, 0], dst_ref=gx.at[j], send_sem=send2.at[j], recv_sem=recv2.at[j],
            device_id=net.twin(), device_id_type=MESH,
        )

        @pl.when(jnp.logical_or(to_core != core, here != j))
        def _():
            made.wait_recv()

        cols = slice(j * OWN, (j + 1) * OWN)
        s16[:, cols] = res[0, :, cols] + gx[j].astype(f32)[:, 0:OWN]
    for k in range(1, 16):
        away[k].wait_send()

    @pl.when(to_core != core)
    def _():
        away[0].wait_send()

    mig_twin(0)
    mig_twin(1)

    x, t, r = (x0, x1, x2), (t0, t1, t2), (r0, r1, r2)
    ca, cb, bb, aa = (ca0, ca1, ca2), (cb0, cb1, cb2), (bb0, bb1, bb2), (aa0, aa1, aa2)

    stream = s16[...]
    power = jnp.sum(stream * stream, axis=1, keepdims=True)
    sums[0, 0:16] = jnp.broadcast_to(power, (16, 128))
    lane = lax.broadcasted_iota(jnp.int32, (1, 128), 1)
    held = jnp.full((1, 128), -1, jnp.int32)
    for e in range(32):
        at = owner[e]
        held = jnp.where(jnp.logical_or(lane == at, lane == at + 32), e, held)
    share = jnp.zeros((8, 128), jnp.float32)
    for k in range(8):
        share = share + jnp.where(ids[:, k:k + 1] == held, gates[:, k:k + 1], 0.0)
    sums[0, 16:24] = share
    both[pl.ds(pl.multiple_of(core * 8, 8), 8)] = share
    pair = net.copy(sums.at[0], sums.at[1], net.twin())
    accg[...] = jnp.zeros_like(accg)
    accu[...] = jnp.zeros_like(accu)
    pair.wait()
    power = (sums[0, 0:16][:, 0:1] + sums[1, 0:16][:, 0:1]) * (1.0 / WIDE)
    scale = lax.rsqrt(power + norm_eps)
    both[pl.ds(pl.multiple_of((1 - core) * 8, 8), 8)] = sums[1, 16:24]
    share = both[...]
    high = share.astype(jnp.bfloat16)
    rest = (share - high.astype(jnp.float32)).astype(jnp.bfloat16)
    px, py, pz = net.pos
    x[2][px, py, pz, :, 1024:1152] = jnp.where(lane < 32, high, rest)
    for p, (off, width) in enumerate(PARTS):
        cols = slice(off, off + width)
        x[p][px, py, pz, :, 0:width] = (s16[:, cols] * scale * gain[core][:, cols]).astype(jnp.bfloat16)
    ga = []
    for p in range(3):
        block = x[p].at[px, py, pz]
        ga.append([go(block, block, net.near(ORDER[p][0], k)) for k in (1, 3, 2)])
    for made in mt:
        made.wait_recv()
    found = mg[lax.rem(sender, 2), sender // 8, lax.rem(sender // 2, 4)]
    quarter[px] = jnp.where(has_in > 0, found, jnp.zeros_like(found))
    mx = [go(quarter.at[px], quarter.at[px], net.near(0, k)) for k in (1, 3, 2)]

    JS = (0, 1, 3, 2)
    SLOT = {1: 1, 3: 0, 2: 2}
    gb = [None] * 3
    gc = [[None] * 4 for _ in range(3)]
    gf = [[None] * 4 for _ in range(3)]
    twins = []

    def line(p, ref, jb, jc):
        return ref.at[place(p, ALL, net.along(ORDER[p][1], jb), net.along(ORDER[p][2], jc))]

    def to_twin(p, jb, jc):
        made = go(line(p, x[p], jb, jc), line(p, t[p], jb, jc), net.twin())
        twins.append((p, jb, jc, made))

    def spread(p, n):
        src = line(p, x[p], JS[n], 0)
        gc[p][n] = [go(src, src, net.near(ORDER[p][2], k)) for k in (1, 3)]
        to_twin(p, JS[n], 0)

    def multiply(p, ref, jc, half):
        off, width = PARTS[p]
        where = place(p, ALL, ALL, net.along(ORDER[p][2], jc))

        def step(k, carry):
            lanes = pl.ds(pl.multiple_of(k * TILE, TILE), TILE)
            rows = pl.ds(pl.multiple_of(off + k * TILE, TILE), TILE)
            left = ref[where + (ALL, lanes)].reshape(256, TILE)
            accg[where] += jnp.dot(left, wg[half, rows, :], preferred_element_type=jnp.float32).reshape(4, 4, 16, 256)
            accu[where] += jnp.dot(left, wu[half, rows, :], preferred_element_type=jnp.float32).reshape(4, 4, 16, 256)
            return carry

        lax.fori_loop(0, width // TILE, step, 0)

    for p in range(3):
        for made in ga[p]:
            made.wait_recv()
        src = line(p, x[p], 0, 0)
        gb[p] = [go(src, src, net.near(ORDER[p][1], k)) for k in (1, 3, 2)]
        spread(p, 0)
    for made in loads:
        made.wait()
    for n in (1, 2, 3):
        for p in range(3):
            gb[p][SLOT[JS[n]]].wait_recv()
            spread(p, n)
    for n in range(4):
        for p in range(3):
            gc[p][n][0].wait_recv()
            gc[p][n][1].wait_recv()
            if n % 2 == 0:
                src = line(p, x[p], JS[n], 3)
                gf[p][n] = go(src, src, net.near(ORDER[p][2], 1))
            else:
                src = line(p, x[p], JS[n], 1)
                gf[p][n] = go(src, src, net.near(ORDER[p][2], 3))
            to_twin(p, JS[n], 3)
            to_twin(p, JS[n], 1)
            if n == 0:
                multiply(p, x[p], 0, 0)
            if n == 1:
                for q, jb, jc, made in twins:
                    if q == p and jc == 0:
                        made.wait_recv()
                multiply(p, t[p], 0, 1)
    for p in range(3):
        multiply(p, x[p], 1, 0)
        multiply(p, x[p], 3, 0)
        for jc in (1, 3):
            for q, jb, kc, made in twins:
                if q == p and kc == jc:
                    made.wait_recv()
            multiply(p, t[p], jc, 1)
    for p in range(3):
        for n in range(4):
            gf[p][n].wait_recv()
            to_twin(p, JS[n], 2)
        multiply(p, x[p], 2, 0)
    for p in range(3):
        for q, jb, kc, made in twins:
            if q == p and kc == 2:
                made.wait_recv()
        multiply(p, t[p], 2, 1)
    for made in sent:
        made.wait_send()
    sent.clear()

    for made in mx:
        made.wait_recv()
    for i in range(4):
        blocks_out[i] = quarter[i, 0:64]
        scales_out[i] = quarter[i, 64:80, 0:128]
    mine = jnp.logical_or(lane == rank, lane == rank + 32)

    def activate(k, carry):
        g = accg[k].reshape(256, 256)
        u = accu[k].reshape(256, 256)
        c = x[2][k, :, :, :, 1024:1152].reshape(256, 128).astype(jnp.float32)
        c = jnp.sum(jnp.where(mine, c, 0.0), axis=1, keepdims=True)
        hid[k] = (g * jax.nn.sigmoid(g) * u * c).astype(jnp.bfloat16).reshape(4, 4, 16, 256)
        return carry

    lax.fori_loop(0, 4, activate, 0)

    def down_twin(p, jc):
        off, width = PARTS[p]
        where = place(p, ALL, ALL, net.along(ORDER[p][2], jc))

        def step(k, carry):
            lanes = pl.ds(pl.multiple_of(k * TILE, TILE), TILE)
            cols = pl.ds(pl.multiple_of(off + k * TILE, TILE), TILE)
            got = jnp.dot(hid[where].reshape(256, 256), wd[1, :, cols], preferred_element_type=jnp.float32)
            t[p][where + (ALL, lanes)] = got.astype(jnp.bfloat16).reshape(4, 4, 16, TILE)
            return carry

        lax.fori_loop(0, width // TILE, step, 0)
        return go(t[p].at[where + (ALL, pl.ds(0, width))], r[p].at[where], net.twin())

    def down_own(p, jc, made):
        off, width = PARTS[p]
        where = place(p, ALL, ALL, net.along(ORDER[p][2], jc))
        made.wait_recv()

        def step(k, carry):
            lanes = pl.ds(pl.multiple_of(k * TILE, TILE), TILE)
            cols = pl.ds(pl.multiple_of(off + k * TILE, TILE), TILE)
            got = jnp.dot(hid[where].reshape(256, 256), wd[0, :, cols], preferred_element_type=jnp.float32)
            got = got + r[p][where + (ALL, lanes)].reshape(256, TILE).astype(jnp.float32)
            x[p][where + (ALL, lanes)] = got.astype(jnp.bfloat16).reshape(4, 4, 16, TILE)
            return carry

        lax.fori_loop(0, width // TILE, step, 0)

    JB = (2, 1, 3, 0)
    PLUS, MINUS = (0, 3), (1, 2)
    steps = [(p, jc) for jc in (2, 1, 3, 0) for p in range(3)]
    made_twin = {}
    h1, h2 = {}, {}

    def add_line(p, jb, jc, others):
        b, c = net.along(ORDER[p][1], jb), net.along(ORDER[p][2], jc)

        def step(k, carry):
            where = place(p, k, b, c) + (ALL, pl.ds(0, PARTS[p][1]))
            total = x[p][where].astype(jnp.float32)
            for ref, index in others:
                total = total + ref[index + (k,)].astype(jnp.float32)
            x[p][where] = total.astype(jnp.bfloat16)
            return carry

        lax.fori_loop(0, 4, step, 0)

    def out_line(p, jb, jc):
        where = place(p, ALL, net.along(ORDER[p][1], jb), net.along(ORDER[p][2], jc))
        return x[p].at[where + (ALL, pl.ds(0, PARTS[p][1]))]

    def send_c1(p):
        h1[p] = []
        for i, n in enumerate(PLUS):
            h1[p].append(go(out_line(p, JB[n], 2), ca[p].at[0, i], net.near(ORDER[p][2], 1)))
        for i, n in enumerate(MINUS):
            h1[p].append(go(out_line(p, JB[n], 2), ca[p].at[1, i], net.near(ORDER[p][2], 3)))

    def send_c2(p, jc):
        way = 0 if jc == 1 else 1
        mine = PLUS if jc == 1 else MINUS
        for i in range(2):
            h1[p][way * 2 + i].wait_recv()
        for n in range(4):
            if n in mine:
                add_line(p, JB[n], jc, [(ca[p], (way, mine.index(n)))])
            h2[p, way, n] = go(out_line(p, JB[n], jc), cb[p].at[way, n], net.near(ORDER[p][2], jc))

    made_twin[steps[0]] = down_twin(*steps[0])
    for i, (p, jc) in enumerate(steps):
        if i + 1 < len(steps):
            made_twin[steps[i + 1]] = down_twin(*steps[i + 1])
        down_own(p, jc, made_twin[p, jc])
        if jc == 2:
            send_c1(p)
        elif jc != 0:
            send_c2(p, jc)
    hb = [[None] * 4 for _ in range(3)]
    for n in range(3):
        for p in range(3):
            for way in range(2):
                h2[p, way, n].wait_recv()
            add_line(p, JB[n], 0, [(cb[p], (0, n)), (cb[p], (1, n))])
            hb[p][n] = go(out_line(p, JB[n], 0), bb[p].at[n], net.near(ORDER[p][1], JB[n]))
    for p in range(3):
        for way in range(2):
            h2[p, way, 3].wait_recv()
        for n in range(3):
            hb[p][n].wait_recv()
        add_line(p, 0, 0, [(cb[p], (0, 3)), (cb[p], (1, 3))] + [(bb[p], (n,)) for n in range(3)])
    haa = []
    for p in range(3):
        _, mb, mc = (net.pos[axis] for axis in ORDER[p])
        for n, k in enumerate((2, 1, 3)):
            src = x[p].at[place(p, net.along(ORDER[p][0], k), mb, mc) + (ALL, pl.ds(0, PARTS[p][1]))]
            haa.append(go(src, aa[p].at[n], net.near(ORDER[p][0], k)))
    for p, (off, width) in enumerate(PARTS):
        for n in range(3):
            haa[p * 3 + n].wait_recv()
        total = x[p][px, py, pz, :, 0:width].astype(jnp.float32)
        for n in range(3):
            total = total + aa[p][n].astype(jnp.float32)
        fin[0, :, off:off + width] = s16[:, off:off + width] + total
    theirs = fin.at[0, pl.ds(pl.multiple_of((1 - core) * 8, 8), 8)]
    last = net.copy(theirs, fin.at[1, pl.ds(0, 8)], net.twin())
    mine = fin[0, pl.ds(pl.multiple_of(core * 8, 8), 8)]
    out[:, pl.ds(pl.multiple_of(core * HALF, HALF), HALF)] = mine.astype(jnp.bfloat16)
    last.wait_recv()
    out[:, pl.ds(pl.multiple_of((1 - core) * HALF, HALF), HALF)] = fin[1, 0:8].astype(jnp.bfloat16)
    last.wait_send()
    for made in sent:
        made.wait_send()


def layer(
    query, pool, block_scale, table, lengths, migration, value_up, out_weight, residual,
    gain, ids, gates, owner, w_gate, w_up, w_down,
):
    bf, f32 = jnp.bfloat16, jnp.float32
    vm = pl.BlockSpec(memory_space=pltpu.VMEM)
    sm = pl.BlockSpec(memory_space=pltpu.SMEM)
    hbm = pl.BlockSpec(memory_space=pl.ANY)
    head = [pltpu.VMEM((4, 4, 16, 1024), bf)] * 8
    grid = [pltpu.VMEM((4, 4, 4, 16, w), bf) for w in GRIDS]
    slots = 250
    return pl.pallas_call(
        kernel,
        out_shape=(
            jax.ShapeDtypeStruct((8, WIDE), bf),
            jax.ShapeDtypeStruct((4, 64, 576), bf),
            jax.ShapeDtypeStruct((4, 16, 128), bf),
        ),
        in_specs=[vm, hbm, vm, vm, sm, sm, hbm, hbm, vm, vm, vm, vm, sm, hbm, hbm, hbm],
        out_specs=(vm, vm, vm),
        scratch_shapes=grid + grid + [
            pltpu.VMEM((2, HALF, 256), bf),
            pltpu.VMEM((2, HALF, 256), bf),
            pltpu.VMEM((2, 256, HALF), bf),
            pltpu.VMEM((4, 4, 4, 16, 256), f32),
            pltpu.VMEM((4, 4, 4, 16, 256), f32),
            pltpu.VMEM((4, 4, 4, 16, 256), bf),
        ] + [pltpu.VMEM((4, 4, 4, 16, w), bf) for _, w in PARTS]
        + [pltpu.VMEM((2, 2, 4, 16, w), bf) for _, w in PARTS]
        + [pltpu.VMEM((2, 4, 4, 16, w), bf) for _, w in PARTS]
        + [pltpu.VMEM((3, 4, 16, w), bf) for _, w in PARTS]
        + [pltpu.VMEM((3, 16, w), bf) for _, w in PARTS]
        + [
            pltpu.VMEM((2, 24, 128), f32),
            pltpu.VMEM((16, 128), f32),
            pltpu.VMEM((2, 16, HALF), f32),
            pltpu.VMEM((4, 4, 576, 128), bf),
            pltpu.VMEM((144, 128), bf),
            pltpu.VMEM((16, 512, 128), bf),
            pltpu.VMEM((256, 2048), bf),
            pltpu.VMEM((4, 512, 128), f32),
        ] + head + [
            pltpu.VMEM((2, 2, 4, 4, 16, 256), f32),
            pltpu.VMEM((4, 4, 4, 16, 256), bf),
            pltpu.VMEM((3, 4, 4, 16, 256), bf),
            pltpu.VMEM((4, 4, 16, 256), bf),
            pltpu.VMEM((16, 16, 256), bf),
            pltpu.VMEM((2, 16, HALF), f32),
            pltpu.VMEM((2, 4, 4, 80, 576), bf),
            pltpu.VMEM((4, 80, 576), bf),
            pltpu.VMEM((8, 1, 1024), f32),
            pltpu.VMEM((64, 576), f32),
            pltpu.VMEM((16, HALF), f32),
            pltpu.SemaphoreType.DMA((12,)),
            pltpu.SemaphoreType.DMA((slots,)),
            pltpu.SemaphoreType.DMA((slots,)),
            pltpu.SemaphoreType.DMA((16,)),
            pltpu.SemaphoreType.DMA((16,)),
        ],
        compiler_params=pltpu.CompilerParams(collective_id=1, has_side_effects=True, vmem_limit_bytes=63 * 2**20),
        name="layer",
    )(
        query, jnp.transpose(pool, (1, 2, 0)), table.T, block_scale.reshape(1, 128), lengths,
        migration.T, value_up, out_weight.T, residual,
        gain.reshape(2, 1, HALF), ids, gates, owner, w_gate, w_up, w_down,
    )


def body(
    query, cache_pool, block_scale, block_table, lengths, migration, value_up, out_weight, residual, norm_gain,
    expert_ids, gate_weights, expert_owner, w_gate, w_up, w_down,
):
    mixed, blocks, scales = layer(
        query, cache_pool, block_scale, block_table, lengths, migration, value_up, out_weight, residual,
        norm_gain, expert_ids, gate_weights, expert_owner, w_gate, w_up, w_down,
    )
    return (mixed, blocks[None], scales[:, 0, 0][None])


def solution(mesh):
    return jax.shard_map(
        body,
        mesh=mesh,
        in_specs=(
            P("dp", "tp", None),
            P("dp", None, None),
            P("dp"),
            P("dp", None),
            P("dp"),
            P(),
            P("tp", None, None),
            P("tp", "dp"),
            P(("dp", "tp"), None),
            P(),
            P(("dp", "tp"), None),
            P(("dp", "tp"), None),
            P(),
            P("dp", None, "tp"),
            P("dp", None, "tp"),
            P("dp", "tp", None),
        ),
        out_specs=(P(("dp", "tp"), None), P("dp", None, None, None), P("dp", None)),
        check_vma=False,
    )
```

```python
import functools
import jax
import jax.numpy as jnp
from jax import lax
from jax.experimental import pallas as pl
from jax.experimental.pallas import tpu as pltpu
from jax.sharding import PartitionSpec as P

MESH = pl.DeviceIdType.MESH
norm_eps = 1e-06
WIDE = 7168
HALF = 3584
PARTS = ((0, 1280), (1280, 1280), (2560, 1024))
GRIDS = (1280, 1280, 1152)
ORDER = ((0, 1, 2), (1, 2, 0), (2, 0, 1))


class Links:
    def __init__(self, send, recv):
        self.send, self.recv, self.used = send, recv, 0
        rank = lax.axis_index("dp")
        self.core = lax.rem(rank, 2)
        self.pos = (lax.axis_index("tp"), rank // 8, lax.rem(rank // 2, 4))

    def device(self, pos, core):
        return ((pos[1] * 4 + pos[2]) * 2 + core, pos[0])

    def along(self, axis, step):
        return lax.rem(self.pos[axis] + step, 4)

    def near(self, axis, step):
        pos = list(self.pos)
        pos[axis] = self.along(axis, step)
        return self.device(pos, self.core)

    def twin(self):
        return self.device(self.pos, 1 - self.core)

    def copy(self, src, dst, device):
        slot = self.used
        self.used += 1
        made = pltpu.make_async_remote_copy(
            src_ref=src,
            dst_ref=dst,
            send_sem=self.send.at[slot],
            recv_sem=self.recv.at[slot],
            device_id=device,
            device_id_type=MESH,
        )
        made.start()
        return made


def place(part, a, b, c):
    index = [None, None, None]
    for axis, value in zip(ORDER[part], (a, b, c)):
        index[axis] = value
    return tuple(index)


ALL = slice(None)


softmax_scale = 192.0 ** (-0.5)
OWN = 224
WITHIN = (((0,), (0,)), ((), ()))
LAST = (((1,), (1,)), ((), ()))
MIG = ((0, 32, 1, 2), (32, 32, 2, 1))


def kernel(
    query, pool, table, scales, lens_s, mig_s, value_up, out_w, residual,
    gain, ids, gates, owner, wg_in, wu_in, wd_in,
    out, blocks_out, scales_out,
    x0, x1, x2, t0, t1, t2, wg, wu, wd, accg, accu, hid,
    r0, r1, r2, ca0, ca1, ca2, cb0, cb1, cb2, bb0, bb1, bb2, aa0, aa1, aa2,
    both, fin,
    kt, hot, vu, wt, lat, h00, h01, h10, h11, n00, n01, n10, n11, part, px_, rx, sp, gx, res, mg, quarter, lane_scale, row, s16,
    load, send, recv, recv2, send2,
):
    keys_in = (t0, t1, r0, r1)
    net = Links(send, recv)
    core = net.core
    x, y, z = net.pos
    rank = (y * 4 + z) * 2 + core
    heads = ((h00, h01), (h10, h11))
    twin_heads = ((n00, n01), (n10, n11))
    f32, bf = jnp.float32, jnp.bfloat16

    def fetch(i, slot):
        return pltpu.make_async_copy(pool.at[pl.ds(i * 4, 4)], kt.at[slot], load.at[slot])

    for i in range(4):
        fetch(i, i).start()
    late = []
    for i, (src, dst) in enumerate(((value_up, vu), (out_w, wt.at[pl.ds(0, OWN)]))):
        made = pltpu.make_async_copy(src, dst, load.at[4 + i])
        made.start()
        late.append(made)

    barrier = pltpu.get_barrier_semaphore()
    for k in range(1, 32):
        other = lax.rem(rank + k, 32)
        pl.semaphore_signal(barrier, inc=1, device_id=(other, x), device_id_type=MESH)
    for k in range(1, 4):
        pl.semaphore_signal(barrier, inc=1, device_id=net.near(0, k), device_id_type=MESH)

    rows = lax.broadcasted_iota(jnp.int32, (32, 128), 0)
    widen = (rows == lax.broadcasted_iota(jnp.int32, (32, 128), 1) // 4).astype(f32)
    names = jnp.dot(table[...].astype(f32), widen, preferred_element_type=f32)
    held = lax.broadcasted_iota(jnp.int32, (4, 128), 0) == lax.rem(lax.broadcasted_iota(jnp.int32, (4, 128), 1), 4)
    names = jnp.sum(jnp.where(held, names, 0.0), axis=0, keepdims=True)
    names = jnp.broadcast_to(names, (128, 128))
    turned = (names == lax.broadcasted_iota(jnp.int32, (128, 128), 0).astype(f32)).astype(f32)
    hot[0:128] = turned.T.astype(bf)
    leaving, sender, has_in = 0, 0, 0
    for i in range(16):
        goes = mig_s[1, i] == rank
        leaving += jnp.where(goes, mig_s[0, i] - rank * 32, 0)
        comes = mig_s[2, i] == rank
        sender += jnp.where(comes, mig_s[1, i], 0)
        has_in += jnp.where(comes, 1, 0)
    slot = leaving * 4 + x
    only = lax.broadcasted_iota(jnp.int32, (128, 128), 0) == slot
    only = jnp.sum(jnp.where(only, hot[0:128].astype(f32), 0.0), axis=0, keepdims=True)
    hot[128:144] = jnp.broadcast_to(only, (16, 128)).astype(bf)
    slot_scale = jnp.dot(jnp.broadcast_to(scales[...].astype(f32), (16, 128)).astype(bf), turned.astype(bf), preferred_element_type=f32)[0:8]
    groups = lax.broadcasted_iota(jnp.int32, (8, 128), 0) == lax.broadcasted_iota(jnp.int32, (8, 128), 1) // 16
    spread = (
        lax.rem(lax.broadcasted_iota(jnp.int32, (128, 1024), 0), 16)
        == lax.rem(lax.broadcasted_iota(jnp.int32, (128, 1024), 1), 16)
    ).astype(bf)
    lane_scale[...] = jnp.dot(jnp.where(groups, slot_scale, 0.0).astype(bf), spread, preferred_element_type=f32).reshape(8, 1, 1024)
    wt[pl.ds(OWN, 32)] = jnp.zeros((32, 2048), bf)
    accg[...] = jnp.zeros_like(accg)
    accu[...] = jnp.zeros_like(accu)
    lane = lax.broadcasted_iota(jnp.int32, (1, 128), 1)
    held = jnp.full((1, 128), -1, jnp.int32)
    for e in range(32):
        at = owner[e]
        held = jnp.where(jnp.logical_or(lane == at, lane == at + 32), e, held)
    share = jnp.zeros((8, 128), f32)
    for k in range(8):
        share = share + jnp.where(ids[:, k:k + 1] == held, gates[:, k:k + 1], 0.0)
    both[pl.ds(pl.multiple_of(core * 8, 8), 8)] = share
    both[pl.ds(pl.multiple_of((1 - core) * 8, 8), 8)] = jnp.zeros((8, 128), f32)

    def turn(i, carry):
        slot = lax.rem(i, 4)
        fetch(i, slot).wait()
        for n in range(4):
            got = lax.dot_general(hot[...], kt[slot, n], LAST, preferred_element_type=f32)
            for g in range(8):
                keys_in[g // 2][i // 4, lax.rem(i, 4), n, :, (g % 2) * 640:(g % 2) * 640 + 576] = got[g * 16:(g + 1) * 16].astype(bf)
            row[pl.ds(i * 4 + n, 1)] = got[128:129]

        @pl.when(i < 12)
        def _():
            fetch(i + 4, slot).start()

        return carry

    lax.fori_loop(0, 16, turn, 0)
    loads = []
    for half in range(2):
        which = core if half == 0 else 1 - core
        rows = pl.ds(pl.multiple_of(which * HALF, HALF), HALF)
        for n, (src, dst) in enumerate(
            ((wg_in.at[0, rows, :], wg.at[half]), (wu_in.at[0, rows, :], wu.at[half]), (wd_in.at[0, :, rows], wd.at[half]))
        ):
            made = pltpu.make_async_copy(src, dst, load.at[6 + half * 3 + n])
            made.start()
            loads.append(made)

    its = jnp.sum(jnp.where(lax.broadcasted_iota(jnp.int32, (8, 128), 1) == slot, slot_scale, 0.0)[0:1], axis=1, keepdims=True)
    mg[core, y, z, :, 0:576] = row[...].astype(bf)
    mg[core, y, z, :, 576:640] = jnp.broadcast_to(its, (64, 64)).astype(bf)

    pl.semaphore_wait(barrier, 34)
    sent = []

    def go(src, dst, device):
        made = net.copy(src, dst, device)
        sent.append(made)
        return made

    mine = residual[:, pl.ds(pl.multiple_of(core * HALF, HALF), HALF)].astype(f32)
    rows = pl.ds(pl.multiple_of(core * 8, 8), 8)
    res[0, rows] = mine
    res[1, rows] = residual[:, pl.ds(pl.multiple_of((1 - core) * HALF, HALF), HALF)].astype(f32)
    swap = go(res.at[1, rows], res.at[0, rows], net.twin())

    def mig_line(i, first):
        off, n, a, b = MIG[i]
        r = pl.ds(off, n)
        return mg.at[core, first, :, r] if a == 2 else mg.at[core, :, first, r]

    m1 = []
    for off, n, a, b in MIG:
        src = mg.at[core, y, z, pl.ds(off, n)]
        m1.append([go(src, src, net.near(a, k)) for k in (1, 3, 2)])
    m2, mt = [None, None], []

    def mig_spread(i):
        off, n, a, b = MIG[i]
        for made in m1[i]:
            made.wait_recv()
        src = mig_line(i, net.pos[b])
        m2[i] = [go(src, src, net.near(b, k)) for k in (1, 3, 2)]
        mt.append(go(src, src, net.twin()))

    def mig_twin(i):
        b = MIG[i][3]
        for k, made in zip((1, 3, 2), m2[i]):
            made.wait_recv()
            src = mig_line(i, net.along(b, 4 - k))
            mt.append(go(src, src, net.twin()))

    def attend(b, k, carry):
        g = b * 2 + k
        q = query[pl.ds(g * 4, 4)].reshape(64, 576)
        keys = keys_in[b][:, :, :, :, pl.ds(pl.multiple_of(k * 640, 640), 576)].reshape(1024, 576)
        scale = lane_scale[g]
        score = lax.dot_general(q, keys, LAST, preferred_element_type=f32)
        lane = lax.broadcasted_iota(jnp.int32, (1, 1024), 1)
        which = lax.rem(lane, 16)
        owner = which // 4
        place_ = lax.rem(which, 4) * 64 + lane // 16
        limit = jnp.where(owner == 0, lens_s[g * 4], jnp.where(owner == 1, lens_s[g * 4 + 1], jnp.where(owner == 2, lens_s[g * 4 + 2], lens_s[g * 4 + 3])))
        holder = jnp.where(place_ < limit, owner, -1)
        live = holder == lax.broadcasted_iota(jnp.int32, (64, 1024), 0) // 16
        score = jnp.where(live, score * (scale * softmax_scale), -1e30)
        top = jnp.max(score, axis=1, keepdims=True)
        expo = jnp.exp(score - top)
        total = jnp.sum(expo, axis=1, keepdims=True)
        coef = (expo * (1.0 / total) * scale).astype(bf)
        got = jnp.dot(coef, keys[:, 0:512], preferred_element_type=f32)
        for n in range(4):
            lat[n, pl.ds(pl.multiple_of(g * 64, 64), 64)] = got[:, n * 128:(n + 1) * 128]
        return carry

    ga = [[None] * 2, [None] * 2]
    gb = [[None] * 2, [None] * 2]
    tw = [[[], []], [[], []]]
    AXES = ((1, 2), (2, 1))

    def value_map(half):
        for h in range(16):
            rows = [lat[n, pl.ds(half * 256 + h, 16, stride=16), :] for n in range(4)]
            rows = jnp.concatenate(rows, axis=1).astype(bf)
            got = jnp.dot(rows, vu[h], preferred_element_type=f32).astype(bf)
            heads[half][h // 8][y, z, :, (h % 8) * 128:(h % 8 + 1) * 128] = got

    def head_line(ref, p, first):
        return ref.at[:, first] if p == 0 else ref.at[first]

    def head_start(half):
        for p in range(2):
            src = heads[half][p].at[y, z]
            ga[half][p] = [go(src, src, net.near(AXES[p][0], k)) for k in (1, 3, 2)]

    def head_twin(half, p, first):
        tw[half][p].append(go(head_line(heads[half][p], p, first), head_line(twin_heads[half][p], p, first), net.twin()))

    def head_spread(half):
        for p in range(2):
            for made in ga[half][p]:
                made.wait_recv()
            first = net.pos[AXES[p][1]]
            src = head_line(heads[half][p], p, first)
            gb[half][p] = [go(src, src, net.near(AXES[p][1], k)) for k in (1, 3, 2)]
            head_twin(half, p, first)

    def head_finish(half):
        for i in range(3):
            for p in range(2):
                gb[half][p][i].wait_recv()
                head_twin(half, p, net.along(AXES[p][1], 4 - (1, 3, 2)[i]))

    def project(half, refs, who):
        total = lax.dot_general(refs[0][...].reshape(256, 1024), wt[:, 0:1024], LAST, preferred_element_type=f32)
        total += lax.dot_general(refs[1][...].reshape(256, 1024), wt[:, 1024:2048], LAST, preferred_element_type=f32)
        part[half, who] = total.reshape(4, 4, 16, 256)

    lax.fori_loop(0, 2, functools.partial(attend, 0), 0)
    lax.fori_loop(0, 2, functools.partial(attend, 1), 0)
    for made in late:
        made.wait()
    value_map(0)
    head_start(0)
    lax.fori_loop(0, 2, functools.partial(attend, 2), 0)
    lax.fori_loop(0, 2, functools.partial(attend, 3), 0)
    value_map(1)
    head_start(1)
    head_spread(0)
    head_spread(1)
    head_finish(0)
    project(0, heads[0], core)
    for p in range(2):
        for made in tw[0][p]:
            made.wait_recv()
    project(0, twin_heads[0], 1 - core)

    def shares(half):
        for n in range(2):
            rows = pl.ds(n * 8, 8)
            both = jnp.concatenate([part[half, 0, :, :, rows], part[half, 1, :, :, rows]], axis=2)
            px_[half * 2 + n] = both.astype(bf)

    shares(0)
    head_finish(1)
    project(1, heads[1], core)
    for p in range(2):
        for made in tw[1][p]:
            made.wait_recv()
    project(1, twin_heads[1], 1 - core)
    shares(1)
    back = [go(px_.at[net.along(0, k)], rx.at[n], net.near(0, k)) for n, k in enumerate((1, 3, 2))]
    mig_spread(0)
    mig_spread(1)
    for made in back:
        made.wait_recv()

    total = px_[x].astype(f32)
    for n in range(3):
        total = total + rx[n].astype(f32)
    sp[...] = total.astype(bf)
    to_core = y // 2
    here = (lax.rem(y, 2) * 4 + z) * 2 + core
    away = []
    for k in range(16):
        ty, tz = net.along(1, k // 4), net.along(2, k % 4)
        made = pltpu.make_async_remote_copy(
            src_ref=sp.at[ty, tz], dst_ref=gx.at[here], send_sem=send2.at[k], recv_sem=recv2.at[here],
            device_id=net.device((x, ty, tz), to_core), device_id_type=MESH,
        )
        away.append(made)
        if k:
            made.start()

    @pl.when(to_core != core)
    def _():
        away[0].start()

    @pl.when(to_core == core)
    def _():
        gx[here] = sp[y, z]

    swap.wait_recv()
    for j in range(16):
        made = pltpu.make_async_remote_copy(
            src_ref=sp.at[0, 0], dst_ref=gx.at[j], send_sem=send2.at[j], recv_sem=recv2.at[j],
            device_id=net.twin(), device_id_type=MESH,
        )

        @pl.when(jnp.logical_or(to_core != core, here != j))
        def _():
            made.wait_recv()

        cols = slice(j * OWN, (j + 1) * OWN)
        s16[:, cols] = res[0, :, cols] + gx[j].astype(f32)[:, 0:OWN]
    for k in range(1, 16):
        away[k].wait_send()

    @pl.when(to_core != core)
    def _():
        away[0].wait_send()

    mig_twin(0)
    mig_twin(1)

    x, t, r = (x0, x1, x2), (t0, t1, t2), (r0, r1, r2)
    ca, cb, bb, aa = (ca0, ca1, ca2), (cb0, cb1, cb2), (bb0, bb1, bb2), (aa0, aa1, aa2)

    stream = s16[...]
    power = jnp.sum(stream * stream, axis=1, keepdims=True)
    lane = lax.broadcasted_iota(jnp.int32, (1, 128), 1)
    px, py, pz = net.pos
    for p, (off, width) in enumerate(PARTS):
        cols = slice(off, off + width)
        x[p][px, py, pz, :, 0:width] = (s16[:, cols] * gain[core][:, cols]).astype(jnp.bfloat16)
    every = both[...]
    first = every.astype(jnp.bfloat16)
    rest = (every - first.astype(jnp.float32)).astype(jnp.bfloat16)
    tops = power.astype(jnp.bfloat16)
    left = power - tops.astype(jnp.float32)
    mids = left.astype(jnp.bfloat16)
    lows = (left - mids.astype(jnp.float32)).astype(jnp.bfloat16)
    extra = jnp.where(lane < 32, first, rest)
    extra = jnp.where(lane == 64, tops, jnp.where(lane == 65, mids, jnp.where(lane == 66, lows, extra)))
    x[2][px, py, pz, :, 1024:1152] = extra
    ga = []
    for p in range(3):
        block = x[p].at[px, py, pz]
        ga.append([go(block, block, net.near(ORDER[p][0], k)) for k in (1, 3, 2)])
    for made in mt:
        made.wait_recv()
    found = mg[lax.rem(sender, 2), sender // 8, lax.rem(sender // 2, 4)]
    quarter[px] = jnp.where(has_in > 0, found, jnp.zeros_like(found))
    mx = [go(quarter.at[px], quarter.at[px], net.near(0, k)) for k in (1, 3, 2)]

    JS = (0, 1, 3, 2)
    gb = [None] * 3
    gc = [[None] * 4 for _ in range(3)]
    gf = [[None] * 4 for _ in range(3)]
    twins = []

    def line(p, ref, jb, jc):
        return ref.at[place(p, ALL, net.along(ORDER[p][1], jb), net.along(ORDER[p][2], jc))]

    def to_twin(p, jb, jc):
        made = go(line(p, x[p], jb, jc), line(p, t[p], jb, jc), net.twin())
        twins.append((p, jb, jc, made))

    def spread(p, n):
        src = line(p, x[p], JS[n], 0)
        gc[p][n] = [go(src, src, net.near(ORDER[p][2], k)) for k in (1, 3)]
        to_twin(p, JS[n], 0)

    def multiply(p, ref, jc, half):
        off, width = PARTS[p]
        where = place(p, ALL, ALL, net.along(ORDER[p][2], jc))

        left = ref[where + (ALL, pl.ds(0, width))].reshape(256, width)
        accg[where] += jnp.dot(left, wg[half, off:off + width, :], preferred_element_type=jnp.float32).reshape(4, 4, 16, 256)
        accu[where] += jnp.dot(left, wu[half, off:off + width, :], preferred_element_type=jnp.float32).reshape(4, 4, 16, 256)

    for p in range(3):
        for made in ga[p]:
            made.wait_recv()
        src = line(p, x[p], 0, 0)
        gb[p] = [go(src, src, net.near(ORDER[p][1], k)) for k in (1, 3)]
    for p in range(3):
        spread(p, 0)
    for made in loads:
        made.wait()
    for p in range(3):
        for k, jb, span in ((3, 1, pl.ds(2, 2)), (1, 3, pl.ds(0, 2))):
            gb[p][0 if k == 1 else 1].wait_recv()
            src = x[p].at[place(p, span, net.along(ORDER[p][1], jb), net.along(ORDER[p][2], 0))]
            gb[p].append(go(src, src, net.near(ORDER[p][1], k)))
        spread(p, 1)
        spread(p, 2)
    for p in range(3):
        for made in gb[p][2:]:
            made.wait_recv()
        spread(p, 3)
    for n in range(4):
        for p in range(3):
            gc[p][n][0].wait_recv()
            gc[p][n][1].wait_recv()
            if n % 2 == 0:
                src = line(p, x[p], JS[n], 3)
                gf[p][n] = go(src, src, net.near(ORDER[p][2], 1))
            else:
                src = line(p, x[p], JS[n], 1)
                gf[p][n] = go(src, src, net.near(ORDER[p][2], 3))
            to_twin(p, JS[n], 3)
            to_twin(p, JS[n], 1)
            if n == 0:
                multiply(p, x[p], 0, 0)
            if n == 1:
                for q, jb, jc, made in twins:
                    if q == p and jc == 0:
                        made.wait_recv()
                multiply(p, t[p], 0, 1)
    for p in range(3):
        multiply(p, x[p], 1, 0)
        multiply(p, x[p], 3, 0)
        for jc in (1, 3):
            for q, jb, kc, made in twins:
                if q == p and kc == jc:
                    made.wait_recv()
            multiply(p, t[p], jc, 1)
    for p in range(3):
        for n in range(4):
            gf[p][n].wait_recv()
            to_twin(p, JS[n], 2)
        multiply(p, x[p], 2, 0)
    for p in range(3):
        for q, jb, kc, made in twins:
            if q == p and kc == 2:
                made.wait_recv()
        multiply(p, t[p], 2, 1)
    for made in sent:
        made.wait_send()
    sent.clear()

    for made in mx:
        made.wait_recv()
    for i in range(4):
        blocks_out[i] = quarter[i, :, 0:576]
        scales_out[i] = quarter[i, 0:16, 512:640]
    mine = jnp.logical_or(lane == rank, lane == rank + 32)

    powers = jnp.logical_and(lane >= 64, lane < 67)

    def activate(k, carry):
        g = accg[k].reshape(256, 256)
        u = accu[k].reshape(256, 256)
        c = x[2][k, :, :, :, 1024:1152].astype(jnp.float32) + t[2][k, :, :, :, 1024:1152].astype(jnp.float32)
        c = c.reshape(256, 128)
        power = jnp.sum(jnp.where(powers, c, 0.0), axis=1, keepdims=True) * (1.0 / WIDE)
        scale = lax.rsqrt(power + norm_eps)
        c = jnp.sum(jnp.where(mine, c, 0.0), axis=1, keepdims=True)
        g = g * scale
        u = u * scale
        hid[k] = (g * jax.nn.sigmoid(g) * u * c).astype(jnp.bfloat16).reshape(4, 4, 16, 256)
        return carry

    lax.fori_loop(0, 4, activate, 0)

    def down_twin(p, jc):
        off, width = PARTS[p]
        where = place(p, ALL, ALL, net.along(ORDER[p][2], jc))
        got = jnp.dot(hid[where].reshape(256, 256), wd[1, :, off:off + width], preferred_element_type=jnp.float32)
        t[p][where + (ALL, pl.ds(0, width))] = got.astype(jnp.bfloat16).reshape(4, 4, 16, width)
        return go(t[p].at[where + (ALL, pl.ds(0, width))], r[p].at[where], net.twin())

    def down_own(p, jc, made):
        off, width = PARTS[p]
        where = place(p, ALL, ALL, net.along(ORDER[p][2], jc))
        made.wait_recv()
        got = jnp.dot(hid[where].reshape(256, 256), wd[0, :, off:off + width], preferred_element_type=jnp.float32)
        got = got + r[p][where].reshape(256, width).astype(jnp.float32)
        x[p][where + (ALL, pl.ds(0, width))] = got.astype(jnp.bfloat16).reshape(4, 4, 16, width)

    JB = (2, 1, 3, 0)
    PLUS, MINUS = (0, 3), (1, 2)
    steps = [(p, jc) for jc in (2, 1, 3, 0) for p in range(3)]
    made_twin = {}
    h1, h2 = {}, {}

    def add_line(p, jb, jc, others):
        b, c = net.along(ORDER[p][1], jb), net.along(ORDER[p][2], jc)
        where = place(p, ALL, b, c) + (ALL, pl.ds(0, PARTS[p][1]))
        total = x[p][where].astype(jnp.float32)
        for ref, index in others:
            total = total + ref[index].astype(jnp.float32)
        x[p][where] = total.astype(jnp.bfloat16)

    def out_line(p, jb, jc):
        where = place(p, ALL, net.along(ORDER[p][1], jb), net.along(ORDER[p][2], jc))
        return x[p].at[where + (ALL, pl.ds(0, PARTS[p][1]))]

    def send_c1(p):
        h1[p] = []
        for i, n in enumerate(PLUS):
            h1[p].append(go(out_line(p, JB[n], 2), ca[p].at[0, i], net.near(ORDER[p][2], 1)))
        for i, n in enumerate(MINUS):
            h1[p].append(go(out_line(p, JB[n], 2), ca[p].at[1, i], net.near(ORDER[p][2], 3)))

    def send_c2(p, jc, arrived):
        way = 0 if jc == 1 else 1
        mine = PLUS if jc == 1 else MINUS
        if arrived:
            for i in range(2):
                h1[p][way * 2 + i].wait_recv()
        for n in range(4):
            if (n in mine) == arrived:
                if arrived:
                    add_line(p, JB[n], jc, [(ca[p], (way, mine.index(n)))])
                h2[p, way, n] = go(out_line(p, JB[n], jc), cb[p].at[way, n], net.near(ORDER[p][2], jc))

    made_twin[steps[0]] = down_twin(*steps[0])
    for i, (p, jc) in enumerate(steps):
        if i + 1 < len(steps):
            made_twin[steps[i + 1]] = down_twin(*steps[i + 1])
        down_own(p, jc, made_twin[p, jc])
        if jc == 2:
            send_c1(p)
        elif jc != 0:
            send_c2(p, jc, False)
    for p in range(3):
        for jc in (1, 3):
            send_c2(p, jc, True)
    halves = (pl.ds(0, 2), pl.ds(2, 2))
    hb = [[None] * 3 for _ in range(3)]
    for n in range(3):
        for p in range(3):
            for way in range(2):
                h2[p, way, n].wait_recv()
            add_line(p, JB[n], 0, [(cb[p], (0, n)), (cb[p], (1, n))])
            b, c = net.along(ORDER[p][1], JB[n]), net.along(ORDER[p][2], 0)
            if n == 0:
                hb[p][0] = []
                for span, k in zip(halves, (1, 3)):
                    src = x[p].at[place(p, span, b, c) + (ALL, pl.ds(0, PARTS[p][1]))]
                    hb[p][0].append(go(src, bb[p].at[0, span], net.near(ORDER[p][1], k)))
            else:
                hb[p][0][n - 1].wait_recv()
                where = place(p, halves[n - 1], b, c) + (ALL, pl.ds(0, PARTS[p][1]))
                total = x[p][where].astype(jnp.float32) + bb[p][0, halves[n - 1]].astype(jnp.float32)
                x[p][where] = total.astype(jnp.bfloat16)
                hb[p][n] = go(out_line(p, JB[n], 0), bb[p].at[n], net.near(ORDER[p][1], JB[n]))
    for p in range(3):
        for way in range(2):
            h2[p, way, 3].wait_recv()
        for n in (1, 2):
            hb[p][n].wait_recv()
        add_line(p, 0, 0, [(cb[p], (0, 3)), (cb[p], (1, 3))] + [(bb[p], (n,)) for n in (1, 2)])
    haa = []
    for p in range(3):
        _, mb, mc = (net.pos[axis] for axis in ORDER[p])
        for n, k in enumerate((2, 1, 3)):
            src = x[p].at[place(p, net.along(ORDER[p][0], k), mb, mc) + (ALL, pl.ds(0, PARTS[p][1]))]
            haa.append(go(src, aa[p].at[n], net.near(ORDER[p][0], k)))
    for p, (off, width) in enumerate(PARTS):
        for n in range(3):
            haa[p * 3 + n].wait_recv()
        total = x[p][px, py, pz, :, 0:width].astype(jnp.float32)
        for n in range(3):
            total = total + aa[p][n].astype(jnp.float32)
        fin[0, :, off:off + width] = s16[:, off:off + width] + total
    theirs = fin.at[0, pl.ds(pl.multiple_of((1 - core) * 8, 8), 8)]
    last = net.copy(theirs, fin.at[1, pl.ds(0, 8)], net.twin())
    mine = fin[0, pl.ds(pl.multiple_of(core * 8, 8), 8)]
    out[:, pl.ds(pl.multiple_of(core * HALF, HALF), HALF)] = mine.astype(jnp.bfloat16)
    last.wait_recv()
    out[:, pl.ds(pl.multiple_of((1 - core) * HALF, HALF), HALF)] = fin[1, 0:8].astype(jnp.bfloat16)
    last.wait_send()
    for made in sent:
        made.wait_send()


def layer(
    query, pool, block_scale, table, lengths, migration, value_up, out_weight, residual,
    gain, ids, gates, owner, w_gate, w_up, w_down,
):
    bf, f32 = jnp.bfloat16, jnp.float32
    vm = pl.BlockSpec(memory_space=pltpu.VMEM)
    sm = pl.BlockSpec(memory_space=pltpu.SMEM)
    hbm = pl.BlockSpec(memory_space=pl.ANY)
    head = [pltpu.VMEM((4, 4, 16, 1024), bf)] * 8
    grid = [pltpu.VMEM((4, 4, 4, 16, w), bf) for w in GRIDS]
    slots = 250
    return pl.pallas_call(
        kernel,
        out_shape=(
            jax.ShapeDtypeStruct((8, WIDE), bf),
            jax.ShapeDtypeStruct((4, 64, 576), bf),
            jax.ShapeDtypeStruct((4, 16, 128), bf),
        ),
        in_specs=[vm, hbm, vm, vm, sm, sm, hbm, hbm, vm, vm, vm, vm, sm, hbm, hbm, hbm],
        out_specs=(vm, vm, vm),
        scratch_shapes=grid + grid + [
            pltpu.VMEM((2, HALF, 256), bf),
            pltpu.VMEM((2, HALF, 256), bf),
            pltpu.VMEM((2, 256, HALF), bf),
            pltpu.VMEM((4, 4, 4, 16, 256), f32),
            pltpu.VMEM((4, 4, 4, 16, 256), f32),
            pltpu.VMEM((4, 4, 4, 16, 256), bf),
        ] + [pltpu.VMEM((4, 4, 4, 16, w), bf) for _, w in PARTS]
        + [pltpu.VMEM((2, 2, 4, 16, w), bf) for _, w in PARTS]
        + [pltpu.VMEM((2, 4, 4, 16, w), bf) for _, w in PARTS]
        + [pltpu.VMEM((3, 4, 16, w), bf) for _, w in PARTS]
        + [pltpu.VMEM((3, 16, w), bf) for _, w in PARTS]
        + [
            pltpu.VMEM((16, 128), f32),
            pltpu.VMEM((2, 16, HALF), f32),
            pltpu.VMEM((4, 4, 576, 128), bf),
            pltpu.VMEM((144, 128), bf),
            pltpu.VMEM((16, 512, 128), bf),
            pltpu.VMEM((256, 2048), bf),
            pltpu.VMEM((4, 512, 128), f32),
        ] + head + [
            pltpu.VMEM((2, 2, 4, 4, 16, 256), f32),
            pltpu.VMEM((4, 4, 4, 16, 256), bf),
            pltpu.VMEM((3, 4, 4, 16, 256), bf),
            pltpu.VMEM((4, 4, 16, 256), bf),
            pltpu.VMEM((16, 16, 256), bf),
            pltpu.VMEM((2, 16, HALF), f32),
            pltpu.VMEM((2, 4, 4, 64, 640), bf),
            pltpu.VMEM((4, 64, 640), bf),
            pltpu.VMEM((8, 1, 1024), f32),
            pltpu.VMEM((64, 576), f32),
            pltpu.VMEM((16, HALF), f32),
            pltpu.SemaphoreType.DMA((12,)),
            pltpu.SemaphoreType.DMA((slots,)),
            pltpu.SemaphoreType.DMA((slots,)),
            pltpu.SemaphoreType.DMA((16,)),
            pltpu.SemaphoreType.DMA((16,)),
        ],
        compiler_params=pltpu.CompilerParams(collective_id=1, has_side_effects=True, vmem_limit_bytes=63 * 2**20),
        name="layer",
    )(
        query, jnp.transpose(pool, (1, 2, 0)), table.T, block_scale.reshape(1, 128), lengths,
        migration.T, value_up, out_weight.T, residual,
        gain.reshape(2, 1, HALF), ids, gates, owner, w_gate, w_up, w_down,
    )


def finish_kernel(mixed, blocks, scales, mixed_out, blocks_out, scales_out):
    mixed_out[...] = mixed[...]
    blocks_out[0] = blocks[...]
    scales_out[...] = jnp.concatenate([scales[i, 0:1, 64:65] for i in range(4)], axis=1)


def finish(mixed, blocks, scales):
    bf = jnp.bfloat16
    vm = pl.BlockSpec(memory_space=pltpu.VMEM)
    return pl.pallas_call(
        finish_kernel,
        out_shape=(
            jax.ShapeDtypeStruct((8, WIDE), bf),
            jax.ShapeDtypeStruct((1, 4, 64, 576), bf),
            jax.ShapeDtypeStruct((1, 4), bf),
        ),
        in_specs=[vm, vm, vm],
        out_specs=(vm, vm, vm),
        name="finish",
    )(mixed, blocks, scales)


def body(
    query, cache_pool, block_scale, block_table, lengths, migration, value_up, out_weight, residual, norm_gain,
    expert_ids, gate_weights, expert_owner, w_gate, w_up, w_down,
):
    mixed, blocks, scales = layer(
        query, cache_pool, block_scale, block_table, lengths, migration, value_up, out_weight, residual,
        norm_gain, expert_ids, gate_weights, expert_owner, w_gate, w_up, w_down,
    )
    return finish(mixed, blocks, scales)


def solution(mesh):
    return jax.shard_map(
        body,
        mesh=mesh,
        in_specs=(
            P("dp", "tp", None),
            P("dp", None, None),
            P("dp"),
            P("dp", None),
            P("dp"),
            P(),
            P("tp", None, None),
            P("tp", "dp"),
            P(("dp", "tp"), None),
            P(),
            P(("dp", "tp"), None),
            P(("dp", "tp"), None),
            P(),
            P("dp", None, "tp"),
            P("dp", None, "tp"),
            P("dp", "tp", None),
        ),
        out_specs=(P(("dp", "tp"), None), P("dp", None, None, None), P("dp", None)),
        check_vma=False,
    )
```

```python
import functools
import jax
import jax.numpy as jnp
from jax import lax
from jax.experimental import pallas as pl
from jax.experimental.pallas import tpu as pltpu
from jax.sharding import PartitionSpec as P

MESH = pl.DeviceIdType.MESH
norm_eps = 1e-06
WIDE = 7168
HALF = 3584
PARTS = ((0, 1280), (1280, 1280), (2560, 1024))
GRIDS = (1280, 1280, 1152)
ORDER = ((0, 1, 2), (1, 2, 0), (2, 0, 1))


class Links:
    def __init__(self, send, recv):
        self.send, self.recv, self.used = send, recv, 0
        rank = lax.axis_index("dp")
        self.core = lax.rem(rank, 2)
        self.pos = (lax.axis_index("tp"), rank // 8, lax.rem(rank // 2, 4))

    def device(self, pos, core):
        return ((pos[1] * 4 + pos[2]) * 2 + core, pos[0])

    def along(self, axis, step):
        return lax.rem(self.pos[axis] + step, 4)

    def near(self, axis, step):
        pos = list(self.pos)
        pos[axis] = self.along(axis, step)
        return self.device(pos, self.core)

    def twin(self):
        return self.device(self.pos, 1 - self.core)

    def copy(self, src, dst, device):
        slot = self.used
        self.used += 1
        made = pltpu.make_async_remote_copy(
            src_ref=src,
            dst_ref=dst,
            send_sem=self.send.at[slot],
            recv_sem=self.recv.at[slot],
            device_id=device,
            device_id_type=MESH,
        )
        made.start()
        return made


def place(part, a, b, c):
    index = [None, None, None]
    for axis, value in zip(ORDER[part], (a, b, c)):
        index[axis] = value
    return tuple(index)


ALL = slice(None)


softmax_scale = 192.0 ** (-0.5)
OWN = 224
WITHIN = (((0,), (0,)), ((), ()))
LAST = (((1,), (1,)), ((), ()))
MIG = ((0, 32, 1, 2), (32, 32, 2, 1))


def kernel(
    query, pool, table, scales, lens_s, mig_s, value_up, out_w, residual,
    gain, ids, gates, owner, wg_in, wu_in, wd_in,
    out, blocks_out, scales_out,
    x0, x1, x2, t0, t1, t2, wg, wu, wd, accg, accu, hid,
    r0, r1, r2, ca0, ca1, ca2, cb0, cb1, cb2, bb0, bb1, bb2, aa0, aa1, aa2,
    both, fin,
    kt, hot, vu, wt, lat, h00, h01, h10, h11, n00, n01, n10, n11, part, px_, rx, sp, gx, res, mg, quarter, lane_scale, row, s16,
    load, send, recv, recv2, send2, recv3, send3,
):
    keys_in = (t0, t1, r0, r1)
    net = Links(send, recv)
    core = net.core
    x, y, z = net.pos
    rank = (y * 4 + z) * 2 + core
    heads = ((h00, h01), (h10, h11))
    twin_heads = ((n00, n01), (n10, n11))
    f32, bf = jnp.float32, jnp.bfloat16

    def fetch(i, slot):
        return pltpu.make_async_copy(pool.at[pl.ds(i * 4, 4)], kt.at[slot], load.at[slot])

    for i in range(4):
        fetch(i, i).start()
    late = []
    for i, (src, dst) in enumerate(((value_up, vu), (out_w, wt.at[pl.ds(0, OWN)]))):
        made = pltpu.make_async_copy(src, dst, load.at[4 + i])
        made.start()
        late.append(made)

    barrier = pltpu.get_barrier_semaphore()
    for k in range(1, 32):
        other = lax.rem(rank + k, 32)
        pl.semaphore_signal(barrier, inc=1, device_id=(other, x), device_id_type=MESH)
    for k in range(1, 4):
        pl.semaphore_signal(barrier, inc=1, device_id=net.near(0, k), device_id_type=MESH)

    rows = lax.broadcasted_iota(jnp.int32, (32, 128), 0)
    widen = (rows == lax.broadcasted_iota(jnp.int32, (32, 128), 1) // 4).astype(f32)
    names = jnp.dot(table[...].astype(f32), widen, preferred_element_type=f32)
    held = lax.broadcasted_iota(jnp.int32, (4, 128), 0) == lax.rem(lax.broadcasted_iota(jnp.int32, (4, 128), 1), 4)
    names = jnp.sum(jnp.where(held, names, 0.0), axis=0, keepdims=True)
    names = jnp.broadcast_to(names, (128, 128))
    turned = (names == lax.broadcasted_iota(jnp.int32, (128, 128), 0).astype(f32)).astype(f32)
    hot[0:128] = turned.T.astype(bf)
    leaving, sender, has_in = 0, 0, 0
    for i in range(16):
        goes = mig_s[1, i] == rank
        leaving += jnp.where(goes, mig_s[0, i] - rank * 32, 0)
        comes = mig_s[2, i] == rank
        sender += jnp.where(comes, mig_s[1, i], 0)
        has_in += jnp.where(comes, 1, 0)
    slot = leaving * 4 + x
    only = lax.broadcasted_iota(jnp.int32, (128, 128), 0) == slot
    only = jnp.sum(jnp.where(only, hot[0:128].astype(f32), 0.0), axis=0, keepdims=True)
    hot[128:144] = jnp.broadcast_to(only, (16, 128)).astype(bf)
    slot_scale = jnp.dot(jnp.broadcast_to(scales[...].astype(f32), (16, 128)).astype(bf), turned.astype(bf), preferred_element_type=f32)[0:8]
    groups = lax.broadcasted_iota(jnp.int32, (8, 128), 0) == lax.broadcasted_iota(jnp.int32, (8, 128), 1) // 16
    spread = (
        lax.rem(lax.broadcasted_iota(jnp.int32, (128, 1024), 0), 16)
        == lax.rem(lax.broadcasted_iota(jnp.int32, (128, 1024), 1), 16)
    ).astype(bf)
    lane_scale[...] = jnp.dot(jnp.where(groups, slot_scale, 0.0).astype(bf), spread, preferred_element_type=f32).reshape(8, 1, 1024)
    wt[pl.ds(OWN, 32)] = jnp.zeros((32, 2048), bf)
    accg[...] = jnp.zeros_like(accg)
    accu[...] = jnp.zeros_like(accu)
    lane = lax.broadcasted_iota(jnp.int32, (1, 128), 1)
    held = jnp.full((1, 128), -1, jnp.int32)
    for e in range(32):
        at = owner[e]
        held = jnp.where(jnp.logical_or(lane == at, lane == at + 32), e, held)
    share = jnp.zeros((8, 128), f32)
    for k in range(8):
        share = share + jnp.where(ids[:, k:k + 1] == held, gates[:, k:k + 1], 0.0)
    both[pl.ds(pl.multiple_of(core * 8, 8), 8)] = share
    both[pl.ds(pl.multiple_of((1 - core) * 8, 8), 8)] = jnp.zeros((8, 128), f32)

    def turn(i, carry):
        slot = lax.rem(i, 4)
        fetch(i, slot).wait()
        for n in range(4):
            got = lax.dot_general(hot[...], kt[slot, n], LAST, preferred_element_type=f32)
            for g in range(8):
                keys_in[g // 2][i // 4, lax.rem(i, 4), n, :, (g % 2) * 640:(g % 2) * 640 + 576] = got[g * 16:(g + 1) * 16].astype(bf)
            row[pl.ds(i * 4 + n, 1)] = got[128:129]

        @pl.when(i < 12)
        def _():
            fetch(i + 4, slot).start()

        return carry

    lax.fori_loop(0, 16, turn, 0)
    loads = []
    for half in range(2):
        which = core if half == 0 else 1 - core
        rows = pl.ds(pl.multiple_of(which * HALF, HALF), HALF)
        for n, (src, dst) in enumerate(
            ((wg_in.at[0, rows, :], wg.at[half]), (wu_in.at[0, rows, :], wu.at[half]), (wd_in.at[0, :, rows], wd.at[half]))
        ):
            made = pltpu.make_async_copy(src, dst, load.at[6 + half * 3 + n])
            made.start()
            loads.append(made)

    its = jnp.sum(jnp.where(lax.broadcasted_iota(jnp.int32, (8, 128), 1) == slot, slot_scale, 0.0)[0:1], axis=1, keepdims=True)
    mg[core, y, z, :, 0:576] = row[...].astype(bf)
    mg[core, y, z, :, 576:640] = jnp.broadcast_to(its, (64, 64)).astype(bf)

    pl.semaphore_wait(barrier, 34)
    sent = []

    def go(src, dst, device):
        made = net.copy(src, dst, device)
        sent.append(made)
        return made

    mine = residual[:, pl.ds(pl.multiple_of(core * HALF, HALF), HALF)].astype(f32)
    rows = pl.ds(pl.multiple_of(core * 8, 8), 8)
    res[0, rows] = mine
    res[1, rows] = residual[:, pl.ds(pl.multiple_of((1 - core) * HALF, HALF), HALF)].astype(f32)
    swap = go(res.at[1, rows], res.at[0, rows], net.twin())

    def mig_line(i, first):
        off, n, a, b = MIG[i]
        r = pl.ds(off, n)
        return mg.at[core, first, :, r] if a == 2 else mg.at[core, :, first, r]

    m1 = []
    for off, n, a, b in MIG:
        src = mg.at[core, y, z, pl.ds(off, n)]
        m1.append([go(src, src, net.near(a, k)) for k in (1, 3, 2)])
    m2, mt = [None, None], []

    def mig_spread(i):
        off, n, a, b = MIG[i]
        for made in m1[i]:
            made.wait_recv()
        src = mig_line(i, net.pos[b])
        m2[i] = [go(src, src, net.near(b, k)) for k in (1, 3, 2)]
        mt.append(go(src, src, net.twin()))

    def mig_twin(i):
        b = MIG[i][3]
        for k, made in zip((1, 3, 2), m2[i]):
            made.wait_recv()
            src = mig_line(i, net.along(b, 4 - k))
            mt.append(go(src, src, net.twin()))

    def attend(b, k, carry):
        g = b * 2 + k
        q = query[pl.ds(g * 4, 4)].reshape(64, 576)
        keys = keys_in[b][:, :, :, :, pl.ds(pl.multiple_of(k * 640, 640), 576)].reshape(1024, 576)
        scale = lane_scale[g]
        score = lax.dot_general(q, keys, LAST, preferred_element_type=f32)
        lane = lax.broadcasted_iota(jnp.int32, (1, 1024), 1)
        which = lax.rem(lane, 16)
        owner = which // 4
        place_ = lax.rem(which, 4) * 64 + lane // 16
        limit = jnp.where(owner == 0, lens_s[g * 4], jnp.where(owner == 1, lens_s[g * 4 + 1], jnp.where(owner == 2, lens_s[g * 4 + 2], lens_s[g * 4 + 3])))
        holder = jnp.where(place_ < limit, owner, -1)
        live = holder == lax.broadcasted_iota(jnp.int32, (64, 1024), 0) // 16
        score = jnp.where(live, score * (scale * softmax_scale), -1e30)
        top = jnp.max(score, axis=1, keepdims=True)
        expo = jnp.exp(score - top)
        total = jnp.sum(expo, axis=1, keepdims=True)
        coef = (expo * (1.0 / total) * scale).astype(bf)
        got = jnp.dot(coef, keys[:, 0:512], preferred_element_type=f32)
        for n in range(4):
            lat[n, pl.ds(pl.multiple_of(g * 64, 64), 64)] = got[:, n * 128:(n + 1) * 128]
        return carry

    ga = [[None] * 2, [None] * 2]
    gb = [[None] * 2, [None] * 2]
    tw = [[[], []], [[], []]]
    AXES = ((1, 2), (2, 1))

    def value_map(half):
        for h in range(16):
            rows = [lat[n, pl.ds(half * 256 + h, 16, stride=16), :] for n in range(4)]
            rows = jnp.concatenate(rows, axis=1).astype(bf)
            got = jnp.dot(rows, vu[h], preferred_element_type=f32).astype(bf)
            heads[half][h // 8][y, z, :, (h % 8) * 128:(h % 8 + 1) * 128] = got

    def head_line(ref, p, first):
        return ref.at[:, first] if p == 0 else ref.at[first]

    def head_start(half):
        for p in range(2):
            src = heads[half][p].at[y, z]
            ga[half][p] = [go(src, src, net.near(AXES[p][0], k)) for k in (1, 3, 2)]

    def head_twin(half, p, first):
        tw[half][p].append(go(head_line(heads[half][p], p, first), head_line(twin_heads[half][p], p, first), net.twin()))

    def head_spread(half):
        for p in range(2):
            for made in ga[half][p]:
                made.wait_recv()
            first = net.pos[AXES[p][1]]
            src = head_line(heads[half][p], p, first)
            gb[half][p] = [go(src, src, net.near(AXES[p][1], k)) for k in (1, 3, 2)]
            head_twin(half, p, first)

    def head_finish(half):
        for i in range(3):
            for p in range(2):
                gb[half][p][i].wait_recv()
                head_twin(half, p, net.along(AXES[p][1], 4 - (1, 3, 2)[i]))

    def project(half, refs, who):
        total = lax.dot_general(refs[0][...].reshape(256, 1024), wt[:, 0:1024], LAST, preferred_element_type=f32)
        total += lax.dot_general(refs[1][...].reshape(256, 1024), wt[:, 1024:2048], LAST, preferred_element_type=f32)
        part[half, who] = total.reshape(4, 4, 16, 256)

    lax.fori_loop(0, 2, functools.partial(attend, 0), 0)
    lax.fori_loop(0, 2, functools.partial(attend, 1), 0)
    for made in late:
        made.wait()
    value_map(0)
    head_start(0)
    lax.fori_loop(0, 2, functools.partial(attend, 2), 0)
    lax.fori_loop(0, 2, functools.partial(attend, 3), 0)
    value_map(1)
    head_start(1)
    head_spread(0)
    head_spread(1)
    head_finish(0)
    project(0, heads[0], core)
    for p in range(2):
        for made in tw[0][p]:
            made.wait_recv()
    project(0, twin_heads[0], 1 - core)

    back = []

    def shares(half):
        for n in range(2):
            rows = pl.ds(n * 8, 8)
            both = jnp.concatenate([part[half, 0, :, :, rows], part[half, 1, :, :, rows]], axis=2)
            px_[half * 2 + n] = both.astype(bf)
        for n in range(2):
            target = half * 2 + n
            slot = lax.rem(target + 7 - x, 4)
            made = pltpu.make_async_remote_copy(
                src_ref=px_.at[target], dst_ref=rx.at[slot], send_sem=send3.at[target], recv_sem=recv3.at[slot],
                device_id=net.device((target, y, z), core), device_id_type=MESH,
            )
            back.append(made)

            @pl.when(target != x)
            def _():
                made.start()

    shares(0)
    head_finish(1)
    project(1, heads[1], core)
    for p in range(2):
        for made in tw[1][p]:
            made.wait_recv()
    project(1, twin_heads[1], 1 - core)
    shares(1)
    mig_spread(0)
    mig_spread(1)
    for n in range(3):
        pltpu.make_async_remote_copy(
            src_ref=px_.at[0], dst_ref=rx.at[n], send_sem=send3.at[0], recv_sem=recv3.at[n],
            device_id=net.near(0, 1), device_id_type=MESH,
        ).wait_recv()

    total = px_[x].astype(f32)
    for n in range(3):
        total = total + rx[n].astype(f32)
    sp[...] = total.astype(bf)
    to_core = y // 2
    here = (lax.rem(y, 2) * 4 + z) * 2 + core
    away = []
    for k in range(16):
        ty, tz = net.along(1, k // 4), net.along(2, k % 4)
        made = pltpu.make_async_remote_copy(
            src_ref=sp.at[ty, tz], dst_ref=gx.at[here], send_sem=send2.at[k], recv_sem=recv2.at[here],
            device_id=net.device((x, ty, tz), to_core), device_id_type=MESH,
        )
        away.append(made)
        if k:
            made.start()

    @pl.when(to_core != core)
    def _():
        away[0].start()

    @pl.when(to_core == core)
    def _():
        gx[here] = sp[y, z]

    swap.wait_recv()
    for j in range(16):
        made = pltpu.make_async_remote_copy(
            src_ref=sp.at[0, 0], dst_ref=gx.at[j], send_sem=send2.at[j], recv_sem=recv2.at[j],
            device_id=net.twin(), device_id_type=MESH,
        )

        @pl.when(jnp.logical_or(to_core != core, here != j))
        def _():
            made.wait_recv()

        cols = slice(j * OWN, (j + 1) * OWN)
        s16[:, cols] = res[0, :, cols] + gx[j].astype(f32)[:, 0:OWN]
    for k in range(1, 16):
        away[k].wait_send()

    @pl.when(to_core != core)
    def _():
        away[0].wait_send()

    for target in range(4):

        @pl.when(target != x)
        def _():
            back[target].wait_send()

    mig_twin(0)
    mig_twin(1)

    x, t, r = (x0, x1, x2), (t0, t1, t2), (r0, r1, r2)
    ca, cb, bb, aa = (ca0, ca1, ca2), (cb0, cb1, cb2), (bb0, bb1, bb2), (aa0, aa1, aa2)

    stream = s16[...]
    power = jnp.sum(stream * stream, axis=1, keepdims=True)
    lane = lax.broadcasted_iota(jnp.int32, (1, 128), 1)
    px, py, pz = net.pos
    for p, (off, width) in enumerate(PARTS):
        cols = slice(off, off + width)
        x[p][px, py, pz, :, 0:width] = (s16[:, cols] * gain[core][:, cols]).astype(jnp.bfloat16)
    every = both[...]
    first = every.astype(jnp.bfloat16)
    rest = (every - first.astype(jnp.float32)).astype(jnp.bfloat16)
    tops = power.astype(jnp.bfloat16)
    left = power - tops.astype(jnp.float32)
    mids = left.astype(jnp.bfloat16)
    lows = (left - mids.astype(jnp.float32)).astype(jnp.bfloat16)
    extra = jnp.where(lane < 32, first, rest)
    extra = jnp.where(lane == 64, tops, jnp.where(lane == 65, mids, jnp.where(lane == 66, lows, extra)))
    x[2][px, py, pz, :, 1024:1152] = extra
    ga = []
    for p in range(3):
        block = x[p].at[px, py, pz]
        ga.append([go(block, block, net.near(ORDER[p][0], k)) for k in (1, 3, 2)])
    for made in mt:
        made.wait_recv()
    found = mg[lax.rem(sender, 2), sender // 8, lax.rem(sender // 2, 4)]
    quarter[px] = jnp.where(has_in > 0, found, jnp.zeros_like(found))

    JS = (0, 1, 3, 2)
    gb = [None] * 3
    gc = [[None] * 4 for _ in range(3)]
    gf = [[None] * 4 for _ in range(3)]
    twins = []

    def line(p, ref, jb, jc):
        return ref.at[place(p, ALL, net.along(ORDER[p][1], jb), net.along(ORDER[p][2], jc))]

    def to_twin(p, jb, jc):
        made = go(line(p, x[p], jb, jc), line(p, t[p], jb, jc), net.twin())
        twins.append((p, jb, jc, made))

    def spread(p, n):
        src = line(p, x[p], JS[n], 0)
        gc[p][n] = [go(src, src, net.near(ORDER[p][2], k)) for k in (1, 3)]
        to_twin(p, JS[n], 0)

    def multiply(p, ref, jc, half):
        off, width = PARTS[p]
        where = place(p, ALL, ALL, net.along(ORDER[p][2], jc))

        left = ref[where + (ALL, pl.ds(0, width))].reshape(256, width)
        accg[where] += jnp.dot(left, wg[half, off:off + width, :], preferred_element_type=jnp.float32).reshape(4, 4, 16, 256)
        accu[where] += jnp.dot(left, wu[half, off:off + width, :], preferred_element_type=jnp.float32).reshape(4, 4, 16, 256)

    for p in range(3):
        for made in ga[p]:
            made.wait_recv()
        src = line(p, x[p], 0, 0)
        gb[p] = [go(src, src, net.near(ORDER[p][1], k)) for k in (1, 3)]
    for p in range(3):
        spread(p, 0)
    for made in loads:
        made.wait()
    for p in range(3):
        for k, jb, span in ((3, 1, pl.ds(2, 2)), (1, 3, pl.ds(0, 2))):
            gb[p][0 if k == 1 else 1].wait_recv()
            src = x[p].at[place(p, span, net.along(ORDER[p][1], jb), net.along(ORDER[p][2], 0))]
            gb[p].append(go(src, src, net.near(ORDER[p][1], k)))
        spread(p, 1)
        spread(p, 2)
    for p in range(3):
        for made in gb[p][2:]:
            made.wait_recv()
        spread(p, 3)
    for n in range(4):
        for p in range(3):
            gc[p][n][0].wait_recv()
            gc[p][n][1].wait_recv()
            if n % 2 == 0:
                src = line(p, x[p], JS[n], 3)
                gf[p][n] = go(src, src, net.near(ORDER[p][2], 1))
            else:
                src = line(p, x[p], JS[n], 1)
                gf[p][n] = go(src, src, net.near(ORDER[p][2], 3))
            to_twin(p, JS[n], 3)
            to_twin(p, JS[n], 1)
        for p in range(3):
            if n == 0:
                multiply(p, x[p], 0, 0)
            if n == 1:
                for q, jb, jc, made in twins:
                    if q == p and jc == 0:
                        made.wait_recv()
                multiply(p, t[p], 0, 1)
    for p in range(3):
        multiply(p, x[p], 1, 0)
        multiply(p, x[p], 3, 0)
        for jc in (1, 3):
            for q, jb, kc, made in twins:
                if q == p and kc == jc:
                    made.wait_recv()
            multiply(p, t[p], jc, 1)
    for p in range(3):
        for n in range(4):
            gf[p][n].wait_recv()
            to_twin(p, JS[n], 2)
    for p in range(3):
        multiply(p, x[p], 2, 0)
    for p in range(3):
        for q, jb, kc, made in twins:
            if q == p and kc == 2:
                made.wait_recv()
        multiply(p, t[p], 2, 1)
    for made in sent:
        made.wait_send()
    sent.clear()
    mx = [go(quarter.at[px], quarter.at[px], net.near(0, k)) for k in (1, 3, 2)]

    mine = jnp.logical_or(lane == rank, lane == rank + 32)

    powers = jnp.logical_and(lane >= 64, lane < 67)

    def activate(k, carry):
        g = accg[k].reshape(256, 256)
        u = accu[k].reshape(256, 256)
        c = x[2][k, :, :, :, 1024:1152].astype(jnp.float32) + t[2][k, :, :, :, 1024:1152].astype(jnp.float32)
        c = c.reshape(256, 128)
        power = jnp.sum(jnp.where(powers, c, 0.0), axis=1, keepdims=True) * (1.0 / WIDE)
        scale = lax.rsqrt(power + norm_eps)
        c = jnp.sum(jnp.where(mine, c, 0.0), axis=1, keepdims=True)
        g = g * scale
        u = u * scale
        hid[k] = (g * jax.nn.sigmoid(g) * u * c).astype(jnp.bfloat16).reshape(4, 4, 16, 256)
        return carry

    lax.fori_loop(0, 4, activate, 0)

    def down_twin(p, jc):
        off, width = PARTS[p]
        where = place(p, ALL, ALL, net.along(ORDER[p][2], jc))
        got = jnp.dot(hid[where].reshape(256, 256), wd[1, :, off:off + width], preferred_element_type=jnp.float32)
        t[p][where + (ALL, pl.ds(0, width))] = got.astype(jnp.bfloat16).reshape(4, 4, 16, width)
        return go(t[p].at[where + (ALL, pl.ds(0, width))], r[p].at[where], net.twin())

    def down_own(p, jc, made):
        off, width = PARTS[p]
        where = place(p, ALL, ALL, net.along(ORDER[p][2], jc))
        made.wait_recv()
        got = jnp.dot(hid[where].reshape(256, 256), wd[0, :, off:off + width], preferred_element_type=jnp.float32)
        got = got + r[p][where].reshape(256, width).astype(jnp.float32)
        x[p][where + (ALL, pl.ds(0, width))] = got.astype(jnp.bfloat16).reshape(4, 4, 16, width)

    JB = (2, 1, 3, 0)
    PLUS, MINUS = (0, 3), (1, 2)
    steps = [(p, jc) for jc in (2, 1, 3, 0) for p in range(3)]
    made_twin = {}
    h1, h2 = {}, {}

    def add_line(p, jb, jc, others):
        b, c = net.along(ORDER[p][1], jb), net.along(ORDER[p][2], jc)
        where = place(p, ALL, b, c) + (ALL, pl.ds(0, PARTS[p][1]))
        total = x[p][where].astype(jnp.float32)
        for ref, index in others:
            total = total + ref[index].astype(jnp.float32)
        x[p][where] = total.astype(jnp.bfloat16)

    def out_line(p, jb, jc):
        where = place(p, ALL, net.along(ORDER[p][1], jb), net.along(ORDER[p][2], jc))
        return x[p].at[where + (ALL, pl.ds(0, PARTS[p][1]))]

    def send_c1(p):
        h1[p] = []
        for i, n in enumerate(PLUS):
            h1[p].append(go(out_line(p, JB[n], 2), ca[p].at[0, i], net.near(ORDER[p][2], 1)))
        for i, n in enumerate(MINUS):
            h1[p].append(go(out_line(p, JB[n], 2), ca[p].at[1, i], net.near(ORDER[p][2], 3)))

    def send_c2(p, jc, arrived):
        way = 0 if jc == 1 else 1
        mine = PLUS if jc == 1 else MINUS
        if arrived:
            for i in range(2):
                h1[p][way * 2 + i].wait_recv()
        for n in range(4):
            if (n in mine) == arrived:
                if arrived:
                    add_line(p, JB[n], jc, [(ca[p], (way, mine.index(n)))])
                h2[p, way, n] = go(out_line(p, JB[n], jc), cb[p].at[way, n], net.near(ORDER[p][2], jc))

    made_twin[steps[0]] = down_twin(*steps[0])
    for i, (p, jc) in enumerate(steps):
        if i + 1 < len(steps):
            made_twin[steps[i + 1]] = down_twin(*steps[i + 1])
        down_own(p, jc, made_twin[p, jc])
        if jc == 2:
            send_c1(p)
        elif jc != 0:
            send_c2(p, jc, False)
    for p in range(3):
        for jc in (1, 3):
            send_c2(p, jc, True)
    for made in mx:
        made.wait_recv()
    for i in range(4):
        blocks_out[i] = quarter[i, :, 0:576]
        scales_out[i] = quarter[i, 0:16, 512:640]
    halves = (pl.ds(0, 2), pl.ds(2, 2))
    hb = [[None] * 3 for _ in range(3)]
    for n in range(3):
        for p in range(3):
            for way in range(2):
                h2[p, way, n].wait_recv()
            add_line(p, JB[n], 0, [(cb[p], (0, n)), (cb[p], (1, n))])
            b, c = net.along(ORDER[p][1], JB[n]), net.along(ORDER[p][2], 0)
            if n == 0:
                hb[p][0] = []
                for span, k in zip(halves, (1, 3)):
                    src = x[p].at[place(p, span, b, c) + (ALL, pl.ds(0, PARTS[p][1]))]
                    hb[p][0].append(go(src, bb[p].at[0, span], net.near(ORDER[p][1], k)))
            else:
                hb[p][0][n - 1].wait_recv()
                where = place(p, halves[n - 1], b, c) + (ALL, pl.ds(0, PARTS[p][1]))
                total = x[p][where].astype(jnp.float32) + bb[p][0, halves[n - 1]].astype(jnp.float32)
                x[p][where] = total.astype(jnp.bfloat16)
                hb[p][n] = go(out_line(p, JB[n], 0), bb[p].at[n], net.near(ORDER[p][1], JB[n]))
    for p in range(3):
        for way in range(2):
            h2[p, way, 3].wait_recv()
        for n in (1, 2):
            hb[p][n].wait_recv()
        add_line(p, 0, 0, [(cb[p], (0, 3)), (cb[p], (1, 3))] + [(bb[p], (n,)) for n in (1, 2)])
    haa = []
    for p in range(3):
        _, mb, mc = (net.pos[axis] for axis in ORDER[p])
        for n, k in enumerate((2, 1, 3)):
            src = x[p].at[place(p, net.along(ORDER[p][0], k), mb, mc) + (ALL, pl.ds(0, PARTS[p][1]))]
            haa.append(go(src, aa[p].at[n], net.near(ORDER[p][0], k)))
    for p, (off, width) in enumerate(PARTS):
        for n in range(3):
            haa[p * 3 + n].wait_recv()
        total = x[p][px, py, pz, :, 0:width].astype(jnp.float32)
        for n in range(3):
            total = total + aa[p][n].astype(jnp.float32)
        fin[0, :, off:off + width] = s16[:, off:off + width] + total
    theirs = fin.at[0, pl.ds(pl.multiple_of((1 - core) * 8, 8), 8)]
    last = net.copy(theirs, fin.at[1, pl.ds(0, 8)], net.twin())
    mine = fin[0, pl.ds(pl.multiple_of(core * 8, 8), 8)]
    out[:, pl.ds(pl.multiple_of(core * HALF, HALF), HALF)] = mine.astype(jnp.bfloat16)
    last.wait_recv()
    out[:, pl.ds(pl.multiple_of((1 - core) * HALF, HALF), HALF)] = fin[1, 0:8].astype(jnp.bfloat16)
    last.wait_send()
    for made in sent:
        made.wait_send()


def layer(
    query, pool, block_scale, table, lengths, migration, value_up, out_weight, residual,
    gain, ids, gates, owner, w_gate, w_up, w_down,
):
    bf, f32 = jnp.bfloat16, jnp.float32
    vm = pl.BlockSpec(memory_space=pltpu.VMEM)
    sm = pl.BlockSpec(memory_space=pltpu.SMEM)
    hbm = pl.BlockSpec(memory_space=pl.ANY)
    head = [pltpu.VMEM((4, 4, 16, 1024), bf)] * 8
    grid = [pltpu.VMEM((4, 4, 4, 16, w), bf) for w in GRIDS]
    slots = 250
    return pl.pallas_call(
        kernel,
        out_shape=(
            jax.ShapeDtypeStruct((8, WIDE), bf),
            jax.ShapeDtypeStruct((4, 64, 576), bf),
            jax.ShapeDtypeStruct((4, 16, 128), bf),
        ),
        in_specs=[vm, hbm, vm, vm, sm, sm, hbm, hbm, vm, vm, vm, vm, sm, hbm, hbm, hbm],
        out_specs=(vm, vm, vm),
        scratch_shapes=grid + grid + [
            pltpu.VMEM((2, HALF, 256), bf),
            pltpu.VMEM((2, HALF, 256), bf),
            pltpu.VMEM((2, 256, HALF), bf),
            pltpu.VMEM((4, 4, 4, 16, 256), f32),
            pltpu.VMEM((4, 4, 4, 16, 256), f32),
            pltpu.VMEM((4, 4, 4, 16, 256), bf),
        ] + [pltpu.VMEM((4, 4, 4, 16, w), bf) for _, w in PARTS]
        + [pltpu.VMEM((2, 2, 4, 16, w), bf) for _, w in PARTS]
        + [pltpu.VMEM((2, 4, 4, 16, w), bf) for _, w in PARTS]
        + [pltpu.VMEM((3, 4, 16, w), bf) for _, w in PARTS]
        + [pltpu.VMEM((3, 16, w), bf) for _, w in PARTS]
        + [
            pltpu.VMEM((16, 128), f32),
            pltpu.VMEM((2, 16, HALF), f32),
            pltpu.VMEM((4, 4, 576, 128), bf),
            pltpu.VMEM((144, 128), bf),
            pltpu.VMEM((16, 512, 128), bf),
            pltpu.VMEM((256, 2048), bf),
            pltpu.VMEM((4, 512, 128), f32),
        ] + head + [
            pltpu.VMEM((2, 2, 4, 4, 16, 256), f32),
            pltpu.VMEM((4, 4, 4, 16, 256), bf),
            pltpu.VMEM((4, 4, 4, 16, 256), bf),
            pltpu.VMEM((4, 4, 16, 256), bf),
            pltpu.VMEM((16, 16, 256), bf),
            pltpu.VMEM((2, 16, HALF), f32),
            pltpu.VMEM((2, 4, 4, 64, 640), bf),
            pltpu.VMEM((4, 64, 640), bf),
            pltpu.VMEM((8, 1, 1024), f32),
            pltpu.VMEM((64, 576), f32),
            pltpu.VMEM((16, HALF), f32),
            pltpu.SemaphoreType.DMA((12,)),
            pltpu.SemaphoreType.DMA((slots,)),
            pltpu.SemaphoreType.DMA((slots,)),
            pltpu.SemaphoreType.DMA((16,)),
            pltpu.SemaphoreType.DMA((16,)),
            pltpu.SemaphoreType.DMA((4,)),
            pltpu.SemaphoreType.DMA((4,)),
        ],
        compiler_params=pltpu.CompilerParams(collective_id=1, has_side_effects=True, vmem_limit_bytes=63 * 2**20),
        name="layer",
    )(
        query, jnp.transpose(pool, (1, 2, 0)), table.T, block_scale.reshape(1, 128), lengths,
        migration.T, value_up, out_weight.T, residual,
        gain.reshape(2, 1, HALF), ids, gates, owner, w_gate, w_up, w_down,
    )


def finish_kernel(mixed, blocks, scales, mixed_out, blocks_out, scales_out):
    mixed_out[...] = mixed[...]
    blocks_out[0] = blocks[...]
    scales_out[...] = jnp.concatenate([scales[i, 0:1, 64:65] for i in range(4)], axis=1)


def finish(mixed, blocks, scales):
    bf = jnp.bfloat16
    vm = pl.BlockSpec(memory_space=pltpu.VMEM)
    return pl.pallas_call(
        finish_kernel,
        out_shape=(
            jax.ShapeDtypeStruct((8, WIDE), bf),
            jax.ShapeDtypeStruct((1, 4, 64, 576), bf),
            jax.ShapeDtypeStruct((1, 4), bf),
        ),
        in_specs=[vm, vm, vm],
        out_specs=(vm, vm, vm),
        name="finish",
    )(mixed, blocks, scales)


def body(
    query, cache_pool, block_scale, block_table, lengths, migration, value_up, out_weight, residual, norm_gain,
    expert_ids, gate_weights, expert_owner, w_gate, w_up, w_down,
):
    mixed, blocks, scales = layer(
        query, cache_pool, block_scale, block_table, lengths, migration, value_up, out_weight, residual,
        norm_gain, expert_ids, gate_weights, expert_owner, w_gate, w_up, w_down,
    )
    return finish(mixed, blocks, scales)


def solution(mesh):
    return jax.shard_map(
        body,
        mesh=mesh,
        in_specs=(
            P("dp", "tp", None),
            P("dp", None, None),
            P("dp"),
            P("dp", None),
            P("dp"),
            P(),
            P("tp", None, None),
            P("tp", "dp"),
            P(("dp", "tp"), None),
            P(),
            P(("dp", "tp"), None),
            P(("dp", "tp"), None),
            P(),
            P("dp", None, "tp"),
            P("dp", None, "tp"),
            P("dp", "tp", None),
        ),
        out_specs=(P(("dp", "tp"), None), P("dp", None, None, None), P("dp", None)),
        check_vma=False,
    )
```
